32 devices in a mesh: dp: 2 (over y), expert: 16 (over z, x, core).
Axes of the slice: x: 2, y: 2, z: 4, core: 2. Of those that a mesh axis runs over, the one named last changes fastest.
Arguments:
- tokens: bfloat16 [2048, 1024], P(('dp', 'expert')), may hold values from -6 to 6
- expert_ids: int32 [2048, 8], P(('dp', 'expert')), may hold values from 0 to 15, all different within a row; in each aligned block of 64 rows (0 to 63, 64 to 127, ...) at most 40 rows name the same one
- route_weight: float32 [2048, 8], P(('dp', 'expert')), may hold values from 0.05 to 0.5
- out_grad: bfloat16 [2048, 1024], P(('dp', 'expert')), may hold values from -6 to 6
- gate_weight: bfloat16 [16, 1024, 384], P('expert', 'dp'), may hold values from -0.1875 to 0.1875
- up_weight: bfloat16 [16, 1024, 384], P('expert', 'dp'), may hold values from -0.1875 to 0.1875
- down_weight: bfloat16 [16, 384, 1024], P('expert', None, 'dp'), may hold values from -0.3125 to 0.3125
Outputs:
- layer_out: bfloat16 [2048, 1024], P(('dp', 'expert'))
- token_grad: bfloat16 [2048, 1024], P(('dp', 'expert'))
- route_grad: float32 [2048, 8], P(('dp', 'expert'))
- gate_grad: float32 [16, 1024, 384], P('expert', 'dp')
- up_grad: float32 [16, 1024, 384], P('expert', 'dp')
- down_grad: float32 [16, 384, 1024], P('expert', None, 'dp')
The draws below stay inside these ranges and needn't reach their ends.
Inputs may be any that keep to these rules, and one draw needn't show every extreme that they name: `expert_ids`: each token names 8 different experts. Among the 64 tokens of one device no expert is named by more than 40 tokens, and in every draw some expert is named by exactly 40 tokens of some device.
All inputs are finite; a program needn't handle non-finite values.
Results may differ from the reference program's by a relative error of at most 0.012.
Values may be sent and summed in bfloat16 or wider, within the bound.
A program may use at most 64 MiB of HBM per device.

```python
import math
import jax
import jax.numpy as jnp
import numpy as np
from jax import lax

D = 1024
HID = 384
TOP = 8
TOK_DEV = 64
EXPERTS = 16
CAP = 40
TOKENS = 2048
N_DP = 2
N_EXPERT = 16


def shard_levels(key, extent, shards, low, top_value):
    def one(axis_at, blocks):
        heights = jax.random.uniform(jax.random.fold_in(jax.random.fold_in(key, 6), axis_at), (blocks,), jnp.float32, low / len(shards), top_value / len(shards))
        return jnp.repeat(jnp.exp(heights), extent[axis_at] // blocks).reshape((-1,) + (1,) * (len(extent) - axis_at - 1))

    gain = one(*shards[0])
    for cut in shards[1:]:
        gain = gain * one(*cut)
    return gain


def shared_out(stream_key, own, number, rows, count, top, most, lean):
    ranking = jax.random.permutation(stream_key, count)
    heavy_load, ordinary = load_shares(count, rows * top, most, lean, True), load_shares(count, rows * top, most, lean, False)
    places = jnp.arange(count)

    def named(sizes, offset_by):
        used = int((sizes > 0).sum())
        fixed = max(1, used // 4)
        moved = fixed + (places - fixed + offset_by * (used - fixed)) % max(1, count - fixed)
        return jnp.zeros((count,), jnp.int32).at[ranking[jnp.where(places < fixed, places, moved)]].set(jnp.asarray(sizes, jnp.int32))

    sizes = jnp.where(number % 4 == 0, named(heavy_load, number // 4), named(ordinary, number - number // 4 - 1))
    mixed = jax.random.permutation(jax.random.fold_in(own, 3), count)
    source_of, taker = mixed[0:count // 2 * 2:2], mixed[1:count // 2 * 2:2]
    slack = jnp.minimum(sizes[source_of] - 1, most - sizes[taker]) // 2
    slack = jnp.where((source_of == ranking[0]) | (taker == ranking[0]) | (sizes[taker] == 0), 0, jnp.maximum(slack, 0))
    moved = jax.random.randint(jax.random.fold_in(own, 4), (count // 2,), 0, 1 << 20) % (slack + 1)
    sizes = sizes.at[source_of].add(-moved).at[taker].add(moved)
    labels = jnp.searchsorted(jnp.cumsum(sizes), jnp.arange(rows * top), side="right").astype(jnp.int32)
    listing = labels.reshape(top, rows).T
    listing = listing[jax.random.permutation(jax.random.fold_in(own, 1), rows)]
    offset_by = jax.random.randint(jax.random.fold_in(own, 2), (rows, 1), 0, top)
    return jnp.take_along_axis(listing, (jnp.arange(top)[None, :] + offset_by) % top, axis=1)


def load_shares(number_of, total, limit, lean, full):
    portions = [(1 << 20) // math.isqrt(rank ** lean) + 1 for rank in range(1, number_of + 1)]
    largest = limit if full else min(limit, max(-(-total // number_of), total * portions[0] // sum(portions)))
    least = 1 if total - largest >= number_of - 1 else 0
    given, spare = [largest] + [least] * (number_of - 1), total - largest - least * (number_of - 1)
    while spare > 0:
        movable = [i for i in range(1, number_of) if given[i] < largest] or [i for i in range(1, number_of) if given[i] < limit]
        pool, left = sum([portions[i] for i in movable]), spare
        for i in movable:
            more = min(limit - given[i], max(1, left * portions[i] // pool), spare)
            given[i] = given[i] + more
            spare = spare - more
    return np.array(given)


def gaussian(key, dims, scale, limit, split=(), kind=jnp.bfloat16):
    loudness = shard_levels(key, dims, split, -0.22, 0.18) if split else 1.0
    entries = jax.random.normal(key, dims, jnp.float32) * scale * loudness
    return jnp.minimum(jnp.maximum(entries, -limit), limit).astype(kind)


def setup_inputs(seed: int = 0) -> dict:
    key_list = jax.random.split(jax.random.key(seed), 8)
    tokens = gaussian(key_list[0], (TOKENS, D), 1.0, 6.0, ((0, 32),))
    expert_ids_keys = jax.random.split(jax.random.fold_in(key_list[1], 1), TOKENS // TOK_DEV)
    expert_ids_turns = jax.random.permutation(jax.random.fold_in(key_list[1], 3), TOKENS // TOK_DEV)
    expert_ids = jax.vmap(lambda own, number: shared_out(jax.random.fold_in(key_list[1], 2), own, number, TOK_DEV, EXPERTS, TOP, CAP, 1))(expert_ids_keys, expert_ids_turns).reshape((TOKENS, TOP))
    route_weight = jnp.clip(jnp.exp(math.log(0.5) - 2.3025851 * jax.random.uniform(key_list[2], (TOKENS, TOP), jnp.float32) ** shard_levels(key_list[2], (TOKENS, TOP), ((0, 32),), -0.2, 0.2)), 0.05, 0.5)
    out_grad = gaussian(key_list[3], (TOKENS, D), 1.0, 6.0, ((0, 32),))
    gate_weight = gaussian(key_list[4], (EXPERTS, D, HID), D ** -0.5, 0.1875, ((0, 16), (1, 2)))
    up_weight = gaussian(key_list[5], (EXPERTS, D, HID), D ** -0.5, 0.1875, ((0, 16), (1, 2)))
    down_weight = gaussian(key_list[6], (EXPERTS, HID, D), HID ** -0.5, 0.3125, ((0, 16), (2, 2)))
    return {"tokens": tokens, "expert_ids": expert_ids, "route_weight": route_weight, "out_grad": out_grad, "gate_weight": gate_weight, "up_weight": up_weight, "down_weight": down_weight}


def expert_pass(x_rows, dy_rows, gate_w, up_w, down_w):
    gate_act = jnp.dot(x_rows, gate_w, preferred_element_type=jnp.float32)
    up_act = jnp.dot(x_rows, up_w, preferred_element_type=jnp.float32)
    sigmoid_g = jax.nn.sigmoid(gate_act)
    hidden = (gate_act * sigmoid_g * up_act).astype(jnp.bfloat16)
    y_rows = jnp.dot(hidden, down_w, preferred_element_type=jnp.float32).astype(jnp.bfloat16)
    hidden_grad = jnp.dot(dy_rows, down_w.T, preferred_element_type=jnp.float32)
    gate_back = (hidden_grad * up_act * sigmoid_g * (1.0 + gate_act * (1.0 - sigmoid_g))).astype(jnp.bfloat16)
    up_back = (hidden_grad * gate_act * sigmoid_g).astype(jnp.bfloat16)
    x_grad = (jnp.dot(gate_back, gate_w.T, preferred_element_type=jnp.float32)
              + jnp.dot(up_back, up_w.T, preferred_element_type=jnp.float32)).astype(jnp.bfloat16)
    gate_part = jnp.dot(x_rows.T, gate_back, preferred_element_type=jnp.float32).astype(jnp.bfloat16)
    up_part = jnp.dot(x_rows.T, up_back, preferred_element_type=jnp.float32).astype(jnp.bfloat16)
    down_part = jnp.dot(hidden.T, dy_rows, preferred_element_type=jnp.float32).astype(jnp.bfloat16)
    return y_rows, x_grad, gate_part, up_part, down_part


def reference(tokens, expert_ids, route_weight, out_grad, gate_weight, up_weight, down_weight):
    group_rows = TOK_DEV * N_EXPERT
    max_rows = N_EXPERT * CAP
    x_groups = tokens.reshape(N_DP, group_rows, D)
    id_groups = expert_ids.reshape(N_DP, group_rows, TOP)
    weight_groups = route_weight.reshape(N_DP, group_rows, TOP)
    grad_groups = out_grad.reshape(N_DP, group_rows, D)

    def per_group(carry, group):
        x_part, id_part, weight_part, grad_part = group
        flat_ids = id_part.reshape(-1).astype(jnp.int32)
        one_hot = (flat_ids[:, None] == jnp.arange(EXPERTS, dtype=jnp.int32)[None, :]).astype(jnp.int32)
        slot_rank = jnp.sum((jnp.cumsum(one_hot, 0) - one_hot) * one_hot, 1).astype(jnp.int32)
        pair_slots = (flat_ids * max_rows + slot_rank).astype(jnp.int32)
        x_pairs = jnp.repeat(x_part, TOP, 0)
        dy_pairs = (weight_part.reshape(-1, 1) * jnp.repeat(grad_part, TOP, 0).astype(jnp.float32)).astype(jnp.bfloat16)
        x_buffer = jnp.zeros((EXPERTS * max_rows, D), jnp.bfloat16).at[pair_slots].set(x_pairs)
        dy_buffer = jnp.zeros((EXPERTS * max_rows, D), jnp.bfloat16).at[pair_slots].set(dy_pairs)
        x_buffer = x_buffer.reshape(EXPERTS, max_rows, D)
        dy_buffer = dy_buffer.reshape(EXPERTS, max_rows, D)

        def per_expert(items):
            return expert_pass(*items)

        y_buf, dx_buf, gate_part, up_part, down_part = lax.map(
            per_expert, (x_buffer, dy_buffer, gate_weight, up_weight, down_weight))
        y_pairs = y_buf.reshape(-1, D)[pair_slots].reshape(group_rows, TOP, D)
        dx_pairs = dx_buf.reshape(-1, D)[pair_slots].reshape(group_rows, TOP, D)
        layer_part = jnp.sum(weight_part[:, :, None] * y_pairs.astype(jnp.float32), 1).astype(jnp.bfloat16)
        route_part = jnp.sum(grad_part.astype(jnp.float32)[:, None, :] * y_pairs.astype(jnp.float32), 2)
        token_part = jnp.sum(dx_pairs.astype(jnp.float32), 1).astype(jnp.bfloat16)
        new_carry = (carry[0] + gate_part.astype(jnp.float32),
                     carry[1] + up_part.astype(jnp.float32),
                     carry[2] + down_part.astype(jnp.float32))
        return new_carry, (layer_part, token_part, route_part)

    start_carry = (jnp.zeros((EXPERTS, D, HID), jnp.float32),
                   jnp.zeros((EXPERTS, D, HID), jnp.float32),
                   jnp.zeros((EXPERTS, HID, D), jnp.float32))
    grads, stacked = lax.scan(per_group, start_carry, (x_groups, id_groups, weight_groups, grad_groups))
    layer_out = stacked[0].reshape(TOKENS, D)
    token_grad = stacked[1].reshape(TOKENS, D)
    route_grad = stacked[2].reshape(TOKENS, TOP)
    return (layer_out, token_grad, route_grad, grads[0], grads[1], grads[2])
```

```python
import functools

import jax
import jax.numpy as jnp
from jax import lax
from jax.experimental import pallas as pl
from jax.experimental.pallas import tpu as pltpu
from jax.sharding import PartitionSpec as P

MESH = pl.DeviceIdType.MESH
LANES = 128
HALF = 64
F32 = jnp.float32
BF16 = jnp.bfloat16
LAST = (((1,), (1,)), ((), ()))
ROWS = (((0,), (0,)), ((), ()))


def kernel(
    n, m,
    tok, ids, rw, og, gw, uw, dw,
    lo_ref, tg_ref, rg_ref, gg, ug, dg,
    pay, gu, dn, gb, hw, crecv, xrecv, zrecv, gstage, grecv, dstage, drecv,
    brecv_s, usend_s, dsend_s, xsend_s, csend_s, wsend_s, wrecv_s,
    gsend_s, grecv_s, qsend_s, qrecv_s,
    c2send_s, c2recv_s, x2send_s, x2recv_s, z2send_s, z2recv_s,
):
    tb, d_all = tok.shape
    dl, hid = gw.shape[1], gw.shape[2]
    top = ids.shape[1]
    nz = n // 4
    chunk = 4 * tb
    total = n * tb
    me = lax.axis_index("expert")
    dp = lax.axis_index("dp")
    c = me % 2
    x = (me // 2) % 2
    z = me // 4
    xp = me + 2 - 4 * x
    cp = me + 1 - 2 * c

    def rows(b):
        return pl.ds(pl.multiple_of(b * tb, tb), tb)

    def span(d):
        return pl.ds(pl.multiple_of(d * chunk, chunk), chunk)

    def block(zz, xx, cc):
        return zz * 4 + xx * 2 + cc

    def remote(src, dst, send, recv, **where):
        return pltpu.make_async_remote_copy(
            src_ref=src, dst_ref=dst, send_sem=send, recv_sem=recv,
            device_id=where, device_id_type=MESH,
        )

    lane = lax.broadcasted_iota(jnp.int32, (tb, LANES), 1)
    lane_mod = jnp.where(lane < HALF, lane, lane - HALF)
    dense = jnp.zeros((tb, LANES), F32)
    for k in range(top):
        dense = dense + jnp.where(ids[:, k : k + 1] == lane_mod, rw[:, k : k + 1], 0.0)
    hi = dense.astype(BF16).astype(F32)
    pay[rows(me), 0:d_all] = tok[...]
    pay[rows(me), d_all : 2 * d_all] = og[...]
    pay[rows(me), 2 * d_all :] = jnp.where(lane < HALF, hi, dense - hi).astype(BF16)

    barrier = pltpu.get_barrier_semaphore()
    for partner in (xp, cp):
        pl.semaphore_signal(barrier, inc=1, device_id={"expert": partner}, device_id_type=MESH)

    @pl.when(z > 0)
    def _():
        pl.semaphore_signal(barrier, inc=1, device_id={"expert": me - 4}, device_id_type=MESH)

    @pl.when(z < nz - 1)
    def _():
        pl.semaphore_signal(barrier, inc=1, device_id={"expert": me + 4}, device_id_type=MESH)

    for j in range(1, m):
        pl.semaphore_signal(barrier, inc=1, device_id={"dp": (dp + j) % m}, device_id_type=MESH)
    lines = jnp.minimum(z, 1) + jnp.minimum(nz - 1 - z, 1)
    pl.semaphore_wait(barrier, 1 + m + lines)

    my_rows = pl.ds(pl.multiple_of(dp * dl, dl), dl)

    def weight_copies(peer, owner):
        own = pl.ds(pl.multiple_of(owner * dl, dl), dl)
        return (
            remote(gw.at[0], gu.at[own, 0:hid], wsend_s.at[peer, 0], wrecv_s.at[owner, 0], dp=peer),
            remote(uw.at[0], gu.at[own, hid:], wsend_s.at[peer, 1], wrecv_s.at[owner, 1], dp=peer),
            remote(dw.at[0], dn.at[:, own], wsend_s.at[peer, 2], wrecv_s.at[owner, 2], dp=peer),
        )

    for j in range(1, m):
        for copy in weight_copies((dp + j) % m, dp):
            copy.start()

    def gather_copy(b, sem, to):
        return remote(pay.at[rows(b)], pay.at[rows(b)], sem, brecv_s.at[b], expert=to)

    def up(zz):
        return gather_copy(block(zz, x, c), usend_s.at[zz], me + 4)

    def down(zz):
        return gather_copy(block(zz, x, c), dsend_s.at[zz], me - 4)

    def across(zz):
        return gather_copy(block(zz, x, c), xsend_s.at[zz], xp)

    def core(zz, xx):
        return gather_copy(block(zz, xx, c), csend_s.at[zz * 2 + xx], cp)

    def arrived(b):
        gather_copy(b, xsend_s.at[0], xp).wait_recv()

    @pl.when(z < nz - 1)
    def _():
        up(z).start()

    @pl.when(z > 0)
    def _():
        down(z).start()

    across(z).start()
    core(z, x).start()
    gu[my_rows, 0:hid] = gw[0]
    gu[my_rows, hid:] = uw[0]
    dn[:, my_rows] = dw[0]

    def partner_blocks(s):
        @pl.when(s == 0)
        def _():
            arrived(block(z, 1 - x, c))
            core(z, 1 - x).start()

        @pl.when((s > 0) & (z - s >= 0))
        def _():
            arrived(block(z - s, 1 - x, c))
            core(z - s, 1 - x).start()

        @pl.when((s > 0) & (z + s < nz))
        def _():
            arrived(block(z + s, 1 - x, c))
            core(z + s, 1 - x).start()

    def gather_step(s, carry):
        @pl.when(z - s >= 0)
        def _():
            arrived(block(z - s, x, c))

            @pl.when(z < nz - 1)
            def _():
                up(z - s).start()

            across(z - s).start()
            core(z - s, x).start()

        @pl.when(z + s < nz)
        def _():
            arrived(block(z + s, x, c))

            @pl.when(z > 0)
            def _():
                down(z + s).start()

            across(z + s).start()
            core(z + s, x).start()

        partner_blocks(s - 1)
        return carry

    lax.fori_loop(1, nz, gather_step, 0)
    partner_blocks(nz - 1)

    def gather_end(zz, carry):
        arrived(block(zz, 0, 1 - c))
        arrived(block(zz, 1, 1 - c))

        @pl.when((z < nz - 1) & (zz <= z))
        def _():
            up(zz).wait_send()

        @pl.when((z > 0) & (zz >= z))
        def _():
            down(zz).wait_send()

        across(zz).wait_send()
        core(zz, 0).wait_send()
        core(zz, 1).wait_send()
        return carry

    lax.fori_loop(0, nz, gather_end, 0)
    for j in range(1, m):
        other = (dp + j) % m
        for copy in weight_copies(other, other):
            copy.wait_recv()

    wide = lax.broadcasted_iota(jnp.int32, (chunk, LANES), 1)
    mine_hi = wide == me
    mine_lo = wide == me + HALF

    def act_step(r, carry):
        act = jnp.dot(pay[span(r), 0:d_all], gu[...], preferred_element_type=F32)
        raw = lax.dot_general(pay[span(r), d_all : 2 * d_all], dn[...], LAST, preferred_element_type=F32)
        weights = pay[span(r), 2 * d_all :].astype(F32)
        w = jnp.sum(jnp.where(mine_hi | mine_lo, weights, 0.0), 1, keepdims=True)
        gate_act, up_act = act[:, 0:hid], act[:, hid:]
        sig = jax.nn.sigmoid(gate_act)
        silu = gate_act * sig
        hidden = silu * up_act
        hw[span(r), :] = (w * hidden).astype(BF16)
        route = jnp.sum(hidden * raw, 1, keepdims=True)
        route_hi = route.astype(BF16).astype(F32)
        pay[span(r), 2 * d_all :] = jnp.where(
            mine_hi, route_hi, jnp.where(mine_lo, route - route_hi, 0.0)
        ).astype(BF16)
        back = w * raw
        gb[span(r), 0:hid] = (back * up_act * sig * (1.0 + gate_act * (1.0 - sig))).astype(BF16)
        gb[span(r), hid:] = (back * silu).astype(BF16)
        return carry

    lax.fori_loop(0, nz, act_step, 0)

    piece = min(256, dl)
    pieces = dl // piece
    depth = min(total, 1024)

    def contract(left, right):
        def part(i):
            at = pl.ds(i * depth, depth) if isinstance(i, int) else pl.ds(pl.multiple_of(i * depth, depth), depth)
            return lax.dot_general(left(at), right(at), ROWS, preferred_element_type=F32)

        if total == depth:
            return part(0)
        return lax.fori_loop(1, total // depth, lambda i, acc: acc + part(i), part(0))

    def features(owner, i, shift):
        return pl.ds(pl.multiple_of(shift + owner * dl + i * piece, piece), piece)

    def gate_part(owner, i):
        return contract(lambda at: pay[at, features(owner, i, 0)], lambda at: gb[at, :])

    def down_part(owner, i):
        return contract(lambda at: hw[at, :], lambda at: pay[at, features(owner, i, d_all)])

    def cut(i):
        return pl.ds(pl.multiple_of(i * piece, piece), piece)

    def gate_copy(peer, owner, i):
        return remote(
            gstage.at[peer, cut(i)], grecv.at[owner, cut(i)],
            gsend_s.at[peer, i], grecv_s.at[owner, i], dp=peer,
        )

    def down_copy(peer, owner, i):
        return remote(
            dstage.at[peer, i], drecv.at[owner, i], qsend_s.at[peer, i], qrecv_s.at[owner, i], dp=peer
        )

    def share_step(t, carry):
        peer = (dp + 1 + t // pieces) % m
        i = t % pieces
        dstage[peer, i] = down_part(peer, i).astype(BF16)
        down_copy(peer, dp, i).start()
        gstage[peer, cut(i)] = gate_part(peer, i).astype(BF16)
        gate_copy(peer, dp, i).start()
        return carry

    lax.fori_loop(0, (m - 1) * pieces, share_step, 0)

    def own_step(i, carry):
        dg[0, :, cut(i)] = down_part(dp, i)
        own = gate_part(dp, i)
        gg[0, cut(i), :] = own[:, 0:hid]
        ug[0, cut(i), :] = own[:, hid:]
        return carry

    lax.fori_loop(0, pieces, own_step, 0)

    def order(p):
        odd = p % 2
        return (p // 2) * (1 - odd) + (nz - 1 - p // 2) * odd

    def core_back(d, xx):
        return remote(
            pay.at[rows(block(d, xx, 1 - c))], crecv.at[d * 2 + xx],
            c2send_s.at[d * 2 + xx], c2recv_s.at[d * 2 + xx], expert=cp,
        )

    def across_back(d):
        return remote(pay.at[rows(block(d, 1 - x, c))], xrecv.at[d], x2send_s.at[d], x2recv_s.at[d], expert=xp)

    def line_back(d, slot, to):
        return remote(pay.at[rows(block(d, x, c))], zrecv.at[slot], z2send_s.at[d], z2recv_s.at[slot], expert=to)

    def add(b, got):
        pay[rows(b), :] = (pay[rows(b), :].astype(F32) + got[...].astype(F32)).astype(BF16)

    def out_step(p, carry):
        d = order(p)
        pay[span(d), 0:d_all] = jnp.dot(hw[span(d), :], dn[...], preferred_element_type=F32).astype(BF16)
        pay[span(d), d_all : 2 * d_all] = lax.dot_general(
            gb[span(d), :], gu[...], LAST, preferred_element_type=F32
        ).astype(BF16)
        core_back(d, 0).start()
        core_back(d, 1).start()
        return carry

    lax.fori_loop(0, nz, out_step, 0)

    def across_step(p, carry):
        d = order(p)
        core_back(d, 0).wait_recv()
        core_back(d, 1).wait_recv()
        add(block(d, 0, c), crecv.at[d * 2])
        add(block(d, 1, c), crecv.at[d * 2 + 1])
        across_back(d).start()
        return carry

    lax.fori_loop(0, nz, across_step, 0)

    def take_line(d, slot):
        line_back(d, slot, xp).wait_recv()
        add(block(d, x, c), zrecv.at[slot])

    def line_step(p, carry):
        d = order(p)
        across_back(d).wait_recv()
        add(block(d, x, c), xrecv.at[d])

        @pl.when(d < z)
        def _():
            @pl.when(z < nz - 1)
            def _():
                take_line(d, d)

            line_back(d, d, me - 4).start()

        @pl.when(d > z)
        def _():
            @pl.when(z > 0)
            def _():
                take_line(d, d)

            @pl.when(d > z + 1)
            def _():
                line_back(d, d, me + 4).start()

            @pl.when(d == z + 1)
            def _():
                line_back(d, nz, me + 4).start()

        return carry

    lax.fori_loop(0, nz, line_step, 0)

    @pl.when(z < nz - 1)
    def _():
        take_line(z, z)

    @pl.when(z > 0)
    def _():
        take_line(z, nz)

    lo_ref[...] = pay[rows(me), 0:d_all]
    tg_ref[...] = pay[rows(me), d_all : 2 * d_all]
    route = pay[rows(me), 2 * d_all :].astype(F32)
    slot = lax.broadcasted_iota(jnp.int32, (tb, top), 1)
    picked = jnp.zeros((tb, top), F32)
    for k in range(top):
        value = jnp.sum(jnp.where(ids[:, k : k + 1] == lane_mod, route, 0.0), 1, keepdims=True)
        picked = jnp.where(slot == k, value, picked)
    rg_ref[...] = picked

    def share_end(t, carry):
        peer = (dp + 1 + t // pieces) % m
        i = t % pieces
        down_copy(peer, peer, i).wait()
        gate_copy(peer, peer, i).wait()
        dg[0, :, cut(i)] += drecv[peer, i].astype(F32)
        gg[0, cut(i), :] += grecv[peer, cut(i), 0:hid].astype(F32)
        ug[0, cut(i), :] += grecv[peer, cut(i), hid:].astype(F32)
        return carry

    lax.fori_loop(0, (m - 1) * pieces, share_end, 0)

    for j in range(1, m):
        for copy in weight_copies((dp + j) % m, dp):
            copy.wait_send()

    def sends_end(d, carry):
        core_back(d, 0).wait_send()
        core_back(d, 1).wait_send()
        across_back(d).wait_send()

        @pl.when(d != z)
        def _():
            line_back(d, d, xp).wait_send()

        return carry

    lax.fori_loop(0, nz, sends_end, 0)


def shards(tokens, expert_ids, route_weight, out_grad, gate_weight, up_weight, down_weight):
    tb, d_all = tokens.shape
    dl, hid = gate_weight.shape[1:]
    n, m = lax.axis_size("expert"), lax.axis_size("dp")
    nz = n // 4
    total = n * tb
    width = 2 * d_all + LANES
    piece = min(256, dl)
    pieces = dl // piece
    dma = pltpu.SemaphoreType.DMA
    vmem = pl.BlockSpec(memory_space=pltpu.VMEM)
    return tuple(
        pl.pallas_call(
            functools.partial(kernel, n, m),
            out_shape=(
                jax.ShapeDtypeStruct((tb, d_all), BF16),
                jax.ShapeDtypeStruct((tb, d_all), BF16),
                jax.ShapeDtypeStruct(expert_ids.shape, F32),
                jax.ShapeDtypeStruct((1, dl, hid), F32),
                jax.ShapeDtypeStruct((1, dl, hid), F32),
                jax.ShapeDtypeStruct((1, hid, dl), F32),
            ),
            in_specs=[vmem] * 7,
            out_specs=tuple([vmem] * 6),
            scratch_shapes=[
                pltpu.VMEM((total, width), BF16),
                pltpu.VMEM((d_all, 2 * hid), BF16),
                pltpu.VMEM((hid, d_all), BF16),
                pltpu.VMEM((total, 2 * hid), BF16),
                pltpu.VMEM((total, hid), BF16),
                pltpu.VMEM((2 * nz, tb, width), BF16),
                pltpu.VMEM((nz, tb, width), BF16),
                pltpu.VMEM((nz + 1, tb, width), BF16),
                pltpu.VMEM((m, dl, 2 * hid), BF16),
                pltpu.VMEM((m, dl, 2 * hid), BF16),
                pltpu.VMEM((m, pieces, hid, piece), BF16),
                pltpu.VMEM((m, pieces, hid, piece), BF16),
                dma((n,)), dma((nz,)), dma((nz,)), dma((nz,)), dma((2 * nz,)), dma((m, 3)), dma((m, 3)),
                dma((m, pieces)), dma((m, pieces)), dma((m, pieces)), dma((m, pieces)),
                dma((2 * nz,)), dma((2 * nz,)), dma((nz,)), dma((nz,)), dma((nz,)), dma((nz + 1,)),
            ],
            compiler_params=pltpu.CompilerParams(
                collective_id=0, has_side_effects=True, vmem_limit_bytes=60 * 1024 * 1024
            ),
        )(tokens, expert_ids, route_weight, out_grad, gate_weight, up_weight, down_weight)
    )


def solution(mesh):
    rows = P(("dp", "expert"), None)
    return jax.shard_map(
        shards,
        mesh=mesh,
        in_specs=(rows, rows, rows, rows, P("expert", "dp", None), P("expert", "dp", None), P("expert", None, "dp")),
        out_specs=(rows, rows, rows, P("expert", "dp", None), P("expert", "dp", None), P("expert", None, "dp")),
        check_vma=False,
    )
```

```python
import functools

import jax
import jax.numpy as jnp
from jax import lax
from jax.experimental import pallas as pl
from jax.experimental.pallas import tpu as pltpu
from jax.sharding import PartitionSpec as P

MESH = pl.DeviceIdType.MESH
LANES = 128
HALF = 64
F32 = jnp.float32
BF16 = jnp.bfloat16
LAST = (((1,), (1,)), ((), ()))
ROWS = (((0,), (0,)), ((), ()))


def kernel(
    n, m, split,
    tok, ids_t, rw_t, og, gw, uw, dw,
    lo_ref, tg_ref, rg_ref, gg, ug, dg,
    pay, gu, dn, gb, hw, hh, crecv, xrecv, zrecv, gstage, grecv, dstage, drecv,
    brecv_s, usend_s, dsend_s, xsend_s, csend_s, wsend_s, wrecv_s,
    gsend_s, grecv_s, qsend_s, qrecv_s,
    c2send_s, c2recv_s, x2send_s, x2recv_s, z2send_s, z2recv_s,
    *sums,
):
    tb, d_all = tok.shape
    dl, hid = gw.shape[1], gw.shape[2]
    top = ids_t.shape[0]
    yb = sums[0] if split else pay
    nz = n // 4
    chunk = 4 * tb
    total = n * tb
    me = lax.axis_index("expert")
    dp = lax.axis_index("dp")
    c = me % 2
    x = (me // 2) % 2
    z = me // 4
    xp = me + 2 - 4 * x
    cp = me + 1 - 2 * c

    def rows(b):
        return pl.ds(pl.multiple_of(b * tb, tb), tb)

    def span(d):
        return pl.ds(pl.multiple_of(d * chunk, chunk), chunk)

    def block(zz, xx, cc):
        return zz * 4 + xx * 2 + cc

    def remote(src, dst, send, recv, **where):
        return pltpu.make_async_remote_copy(
            src_ref=src, dst_ref=dst, send_sem=send, recv_sem=recv,
            device_id=where, device_id_type=MESH,
        )

    ids = ids_t[...].T
    rw = rw_t[...].T
    lane = lax.broadcasted_iota(jnp.int32, (tb, LANES), 1)
    lane_mod = jnp.where(lane < HALF, lane, lane - HALF)
    dense = jnp.zeros((tb, LANES), F32)
    for k in range(top):
        dense = dense + jnp.where(ids[:, k : k + 1] == lane_mod, rw[:, k : k + 1], 0.0)
    hi = dense.astype(BF16).astype(F32)
    pay[rows(me), 0:d_all] = tok[...]
    pay[rows(me), d_all : 2 * d_all] = og[...]
    pay[rows(me), 2 * d_all :] = jnp.where(lane < HALF, hi, dense - hi).astype(BF16)

    barrier = pltpu.get_barrier_semaphore()
    for partner in (xp, cp):
        pl.semaphore_signal(barrier, inc=1, device_id={"expert": partner}, device_id_type=MESH)

    @pl.when(z > 0)
    def _():
        pl.semaphore_signal(barrier, inc=1, device_id={"expert": me - 4}, device_id_type=MESH)

    @pl.when(z < nz - 1)
    def _():
        pl.semaphore_signal(barrier, inc=1, device_id={"expert": me + 4}, device_id_type=MESH)

    for j in range(1, m):
        pl.semaphore_signal(barrier, inc=1, device_id={"dp": (dp + j) % m}, device_id_type=MESH)
    lines = jnp.minimum(z, 1) + jnp.minimum(nz - 1 - z, 1)
    pl.semaphore_wait(barrier, 1 + m + lines)

    my_rows = pl.ds(pl.multiple_of(dp * dl, dl), dl)

    def weight_copies(peer, owner, which=(0, 1, 2)):
        own = pl.ds(pl.multiple_of(owner * dl, dl), dl)
        ends = (
            (gw.at[0], gu.at[own, 0:hid]),
            (uw.at[0], gu.at[own, hid:]),
            (dw.at[0], dn.at[:, own]),
        )
        return [
            remote(*ends[i], wsend_s.at[peer, i], wrecv_s.at[owner, i], dp=peer) for i in which
        ]

    for j in range(1, m):
        for copy in weight_copies((dp + j) % m, dp, (0, 1)):
            copy.start()

    def gather_copy(b, sem, to):
        return remote(pay.at[rows(b)], pay.at[rows(b)], sem, brecv_s.at[b], expert=to)

    def up(zz):
        return gather_copy(block(zz, x, c), usend_s.at[zz], me + 4)

    def down(zz):
        return gather_copy(block(zz, x, c), dsend_s.at[zz], me - 4)

    def across(zz):
        return gather_copy(block(zz, x, c), xsend_s.at[zz], xp)

    def core(zz, xx):
        return gather_copy(block(zz, xx, c), csend_s.at[zz * 2 + xx], cp)

    def arrived(b):
        gather_copy(b, xsend_s.at[0], xp).wait_recv()

    @pl.when(z < nz - 1)
    def _():
        up(z).start()

    @pl.when(z > 0)
    def _():
        down(z).start()

    across(z).start()
    core(z, x).start()
    gu[my_rows, 0:hid] = gw[0]
    gu[my_rows, hid:] = uw[0]
    dn[:, my_rows] = dw[0]

    def partner_blocks(s):
        @pl.when(s == 0)
        def _():
            arrived(block(z, 1 - x, c))
            core(z, 1 - x).start()

        @pl.when((s > 0) & (z - s >= 0))
        def _():
            arrived(block(z - s, 1 - x, c))
            core(z - s, 1 - x).start()

        @pl.when((s > 0) & (z + s < nz))
        def _():
            arrived(block(z + s, 1 - x, c))
            core(z + s, 1 - x).start()

    def gather_step(s, carry):
        @pl.when(z - s >= 0)
        def _():
            arrived(block(z - s, x, c))

            @pl.when(z < nz - 1)
            def _():
                up(z - s).start()

            across(z - s).start()
            core(z - s, x).start()

        @pl.when(z + s < nz)
        def _():
            arrived(block(z + s, x, c))

            @pl.when(z > 0)
            def _():
                down(z + s).start()

            across(z + s).start()
            core(z + s, x).start()

        partner_blocks(s - 1)
        return carry

    lax.fori_loop(1, nz - 1, gather_step, 0)
    for j in range(1, m):
        weight_copies((dp + j) % m, dp, (2,))[0].start()
    gather_step(nz - 1, 0)

    below, above = z, nz - 1 - z
    upward = jnp.minimum(jnp.maximum(above - below, 0), 1)
    excess = jnp.maximum(above - below, below - above)
    paired = jnp.minimum(above, below)

    def order(p):
        inner = jnp.minimum(jnp.maximum(p - excess + 1, 0), 1)
        q = jnp.maximum(p - excess, 0)
        near = z + (paired - q // 2) * (1 - 2 * (q % 2)) * (2 * upward - 1)
        far = upward * (nz - 1 - p) + (1 - upward) * p
        return inner * near + (1 - inner) * far

    wide = lax.broadcasted_iota(jnp.int32, (chunk, LANES), 1)
    mine_hi = wide == me
    mine_lo = wide == me + HALF

    def chunk_weight(r):
        weights = pay[span(r), 2 * d_all :].astype(F32)
        return jnp.sum(jnp.where(mine_hi | mine_lo, weights, 0.0), 1, keepdims=True)

    def act_step(p, carry):
        r = order(nz - 1 - p)
        arrived(block(r, 0, 1 - c))
        arrived(block(r, 1, 1 - c))
        act = jnp.dot(pay[span(r), 0:d_all], gu[...], preferred_element_type=F32)
        gate_act, up_act = act[:, 0:hid], act[:, hid:]
        sig = jax.nn.sigmoid(gate_act)
        silu = gate_act * sig
        hidden = silu * up_act
        hh[span(r), :] = hidden.astype(BF16)
        hw[span(r), :] = (chunk_weight(r) * hidden).astype(BF16)
        gb[span(r), 0:hid] = (up_act * sig * (1.0 + gate_act * (1.0 - sig))).astype(BF16)
        gb[span(r), hid:] = silu.astype(BF16)
        return carry

    for j in range(1, m):
        other = (dp + j) % m
        for copy in weight_copies(other, other, (0, 1)):
            copy.wait_recv()
    lax.fori_loop(0, nz - 1, act_step, 0)
    partner_blocks(nz - 1)
    act_step(nz - 1, 0)

    def gather_sends(zz, carry):
        @pl.when((z < nz - 1) & (zz <= z))
        def _():
            up(zz).wait_send()

        @pl.when((z > 0) & (zz >= z))
        def _():
            down(zz).wait_send()

        across(zz).wait_send()
        core(zz, 0).wait_send()
        core(zz, 1).wait_send()
        return carry

    def back_step(p, carry):
        r = order(p)
        raw = lax.dot_general(pay[span(r), d_all : 2 * d_all], dn[...], LAST, preferred_element_type=F32)
        back = chunk_weight(r) * raw
        route = jnp.sum(hh[span(r), :].astype(F32) * raw, 1, keepdims=True)
        route_hi = route.astype(BF16).astype(F32)
        yb[span(r), 2 * d_all :] = jnp.where(
            mine_hi, route_hi, jnp.where(mine_lo, route - route_hi, 0.0)
        ).astype(BF16)
        gb[span(r), 0:hid] = (back * gb[span(r), 0:hid].astype(F32)).astype(BF16)
        gb[span(r), hid:] = (back * gb[span(r), hid:].astype(F32)).astype(BF16)
        return carry

    piece = min(256, dl)
    pieces = dl // piece
    depth = min(total, 1024)

    def contract(left, right):
        def part(i):
            at = pl.ds(i * depth, depth) if isinstance(i, int) else pl.ds(pl.multiple_of(i * depth, depth), depth)
            return lax.dot_general(left(at), right(at), ROWS, preferred_element_type=F32)

        if total == depth:
            return part(0)
        return lax.fori_loop(1, total // depth, lambda i, acc: acc + part(i), part(0))

    def features(owner, i, shift):
        return pl.ds(pl.multiple_of(shift + owner * dl + i * piece, piece), piece)

    def gate_part(owner, i):
        return contract(lambda at: pay[at, features(owner, i, 0)], lambda at: gb[at, :])

    def down_part(owner, i):
        return contract(lambda at: hw[at, :], lambda at: pay[at, features(owner, i, d_all)])

    def cut(i):
        return pl.ds(pl.multiple_of(i * piece, piece), piece)

    def gate_copy(peer, owner, i):
        return remote(
            gstage.at[peer, cut(i)], grecv.at[owner, cut(i)],
            gsend_s.at[peer, i], grecv_s.at[owner, i], dp=peer,
        )

    def down_copy(peer, owner, i):
        return remote(
            dstage.at[peer, i], drecv.at[owner, i], qsend_s.at[peer, i], qrecv_s.at[owner, i], dp=peer
        )

    def down_share(t, carry):
        peer = (dp + 1 + t // pieces) % m
        i = t % pieces
        dstage[peer, i] = down_part(peer, i).astype(BF16)
        down_copy(peer, dp, i).start()
        return carry

    def gate_share(t, carry):
        peer = (dp + 1 + t // pieces) % m
        i = t % pieces
        gstage[peer, cut(i)] = gate_part(peer, i).astype(BF16)
        gate_copy(peer, dp, i).start()
        return carry

    def down_own(i, carry):
        dg[0, :, cut(i)] = down_part(dp, i)
        return carry

    def gate_own(i, carry):
        own = gate_part(dp, i)
        gg[0, cut(i), :] = own[:, 0:hid]
        ug[0, cut(i), :] = own[:, hid:]
        return carry

    def core_back(d, xx):
        return remote(
            yb.at[rows(block(d, xx, 1 - c))], crecv.at[d * 2 + xx],
            c2send_s.at[d * 2 + xx], c2recv_s.at[d * 2 + xx], expert=cp,
        )

    def across_back(d):
        return remote(yb.at[rows(block(d, 1 - x, c))], xrecv.at[d], x2send_s.at[d], x2recv_s.at[d], expert=xp)

    def line_back(d, slot, to):
        return remote(yb.at[rows(block(d, x, c))], zrecv.at[slot], z2send_s.at[d], z2recv_s.at[slot], expert=to)

    def add(b, got):
        yb[rows(b), :] = (yb[rows(b), :].astype(F32) + got[...].astype(F32)).astype(BF16)

    def out_step(p, carry):
        d = order(p)
        yb[span(d), 0:d_all] = jnp.dot(hw[span(d), :], dn[...], preferred_element_type=F32).astype(BF16)
        yb[span(d), d_all : 2 * d_all] = lax.dot_general(
            gb[span(d), :], gu[...], LAST, preferred_element_type=F32
        ).astype(BF16)
        core_back(d, 0).start()
        core_back(d, 1).start()
        return carry

    def across_step(p, carry):
        d = order(p)
        core_back(d, 0).wait_recv()
        core_back(d, 1).wait_recv()
        add(block(d, 0, c), crecv.at[d * 2])
        add(block(d, 1, c), crecv.at[d * 2 + 1])
        across_back(d).start()
        return carry

    def take_line(d, slot):
        line_back(d, slot, xp).wait_recv()
        add(block(d, x, c), zrecv.at[slot])

    def line_step(p, carry):
        d = order(p)
        across_back(d).wait_recv()
        add(block(d, x, c), xrecv.at[d])

        @pl.when(d < z)
        def _():
            @pl.when(z < nz - 1)
            def _():
                take_line(d, d)

            line_back(d, d, me - 4).start()

        @pl.when(d > z)
        def _():
            @pl.when(z > 0)
            def _():
                take_line(d, d)

            @pl.when(d > z + 1)
            def _():
                line_back(d, d, me + 4).start()

            @pl.when(d == z + 1)
            def _():
                line_back(d, nz, me + 4).start()

        return carry

    lax.fori_loop(0, (m - 1) * pieces, down_share, 0)
    for j in range(1, m):
        other = (dp + j) % m
        weight_copies(other, other, (2,))[0].wait_recv()

    if split:
        head = min(2, nz)

        def head_step(p, carry):
            back_step(p, carry)
            return out_step(p, carry)

        def tail_step(p, carry):
            out_step(p, carry)
            return across_step(p - 1, carry)

        lax.fori_loop(0, head, head_step, 0)
        lax.fori_loop(head, nz, back_step, 0)
        lax.fori_loop(0, head - 1, across_step, 0)
        lax.fori_loop(0, (m - 1) * pieces, gate_share, 0)
        lax.fori_loop(head, nz, tail_step, 0)
        across_step(nz - 1, 0)
        lax.fori_loop(0, pieces, down_own, 0)
        lax.fori_loop(0, pieces, gate_own, 0)
    else:
        lax.fori_loop(0, nz, gather_sends, 0)
        lax.fori_loop(0, nz, back_step, 0)
        lax.fori_loop(0, (m - 1) * pieces, gate_share, 0)
        lax.fori_loop(0, pieces, down_own, 0)
        lax.fori_loop(0, pieces, gate_own, 0)
        lax.fori_loop(0, nz, out_step, 0)
        lax.fori_loop(0, nz, across_step, 0)

    lax.fori_loop(0, nz, line_step, 0)

    @pl.when(z < nz - 1)
    def _():
        take_line(z, z)

    @pl.when(z > 0)
    def _():
        take_line(z, nz)

    lo_ref[...] = yb[rows(me), 0:d_all]
    tg_ref[...] = yb[rows(me), d_all : 2 * d_all]
    route = yb[rows(me), 2 * d_all :].astype(F32)
    slot = lax.broadcasted_iota(jnp.int32, (tb, top), 1)
    picked = jnp.zeros((tb, top), F32)
    for k in range(top):
        value = jnp.sum(jnp.where(ids[:, k : k + 1] == lane_mod, route, 0.0), 1, keepdims=True)
        picked = jnp.where(slot == k, value, picked)
    rg_ref[...] = picked.T

    def share_end(t, carry):
        peer = (dp + 1 + t // pieces) % m
        i = t % pieces
        down_copy(peer, peer, i).wait()
        gate_copy(peer, peer, i).wait()
        dg[0, :, cut(i)] += drecv[peer, i].astype(F32)
        gg[0, cut(i), :] += grecv[peer, cut(i), 0:hid].astype(F32)
        ug[0, cut(i), :] += grecv[peer, cut(i), hid:].astype(F32)
        return carry

    lax.fori_loop(0, (m - 1) * pieces, share_end, 0)

    for j in range(1, m):
        for copy in weight_copies((dp + j) % m, dp):
            copy.wait_send()
    if split:
        lax.fori_loop(0, nz, gather_sends, 0)

    def sends_end(d, carry):
        core_back(d, 0).wait_send()
        core_back(d, 1).wait_send()
        across_back(d).wait_send()

        @pl.when(d != z)
        def _():
            line_back(d, d, xp).wait_send()

        return carry

    lax.fori_loop(0, nz, sends_end, 0)


def hand_over(*refs):
    count = len(refs) // 2
    sems = refs[-1]
    copies = [pltpu.make_async_copy(refs[i], refs[count + i], sems.at[i]) for i in range(count)]
    for copy in copies:
        copy.start()
    for copy in copies:
        copy.wait()


def shards(tokens, expert_ids, route_weight, out_grad, gate_weight, up_weight, down_weight):
    tb, d_all = tokens.shape
    dl, hid = gate_weight.shape[1:]
    n, m = lax.axis_size("expert"), lax.axis_size("dp")
    nz = n // 4
    total = n * tb
    width = 2 * d_all + LANES
    piece = min(256, dl)
    pieces = dl // piece
    dma = pltpu.SemaphoreType.DMA
    vmem = pl.BlockSpec(memory_space=pltpu.VMEM)
    split = total * width * 2 <= 8 * 1024 * 1024
    results = (
        pl.pallas_call(
            functools.partial(kernel, n, m, split),
            out_shape=(
                jax.ShapeDtypeStruct((tb, d_all), BF16),
                jax.ShapeDtypeStruct((tb, d_all), BF16),
                jax.ShapeDtypeStruct(expert_ids.shape[::-1], F32),
                jax.ShapeDtypeStruct((1, dl, hid), F32),
                jax.ShapeDtypeStruct((1, dl, hid), F32),
                jax.ShapeDtypeStruct((1, hid, dl), F32),
            ),
            in_specs=[vmem] * 7,
            out_specs=tuple([vmem] * 6),
            scratch_shapes=[
                pltpu.VMEM((total, width), BF16),
                pltpu.VMEM((d_all, 2 * hid), BF16),
                pltpu.VMEM((hid, d_all), BF16),
                pltpu.VMEM((total, 2 * hid), BF16),
                pltpu.VMEM((total, hid), BF16),
                pltpu.VMEM((total, hid), BF16),
                pltpu.VMEM((2 * nz, tb, width), BF16),
                pltpu.VMEM((nz, tb, width), BF16),
                pltpu.VMEM((nz + 1, tb, width), BF16),
                pltpu.VMEM((m, dl, 2 * hid), BF16),
                pltpu.VMEM((m, dl, 2 * hid), BF16),
                pltpu.VMEM((m, pieces, hid, piece), BF16),
                pltpu.VMEM((m, pieces, hid, piece), BF16),
                dma((n,)), dma((nz,)), dma((nz,)), dma((nz,)), dma((2 * nz,)), dma((m, 3)), dma((m, 3)),
                dma((m, pieces)), dma((m, pieces)), dma((m, pieces)), dma((m, pieces)),
                dma((2 * nz,)), dma((2 * nz,)), dma((nz,)), dma((nz,)), dma((nz,)), dma((nz + 1,)),
            ]
            + ([pltpu.VMEM((total, width), BF16)] if split else []),
            compiler_params=pltpu.CompilerParams(
                collective_id=0, has_side_effects=True, vmem_limit_bytes=60 * 1024 * 1024
            ),
        )(tokens, expert_ids.T, route_weight.T, out_grad, gate_weight, up_weight, down_weight)
    )
    anywhere = pl.BlockSpec(memory_space=pl.ANY)
    layer_out, token_grad, route_grad, *grads = pl.pallas_call(
        hand_over,
        out_shape=tuple(jax.ShapeDtypeStruct(r.shape, r.dtype) for r in results),
        in_specs=[anywhere] * len(results),
        out_specs=tuple([anywhere] * len(results)),
        scratch_shapes=[dma((len(results),))],
        compiler_params=pltpu.CompilerParams(vmem_limit_bytes=60 * 1024 * 1024),
    )(*results)
    return (layer_out, token_grad, route_grad.T, *grads)


def solution(mesh):
    rows = P(("dp", "expert"), None)
    return jax.shard_map(
        shards,
        mesh=mesh,
        in_specs=(rows, rows, rows, rows, P("expert", "dp", None), P("expert", "dp", None), P("expert", None, "dp")),
        out_specs=(rows, rows, rows, P("expert", "dp", None), P("expert", "dp", None), P("expert", None, "dp")),
        check_vma=False,
    )
```

```python
import functools

import jax
import jax.numpy as jnp
from jax import lax
from jax.experimental import pallas as pl
from jax.experimental.pallas import tpu as pltpu
from jax.sharding import PartitionSpec as P

MESH = pl.DeviceIdType.MESH
LANES = 128
HALF = 64
F32 = jnp.float32
BF16 = jnp.bfloat16
LAST = (((1,), (1,)), ((), ()))
ROWS = (((0,), (0,)), ((), ()))


def kernel(
    n, m, split,
    tok, ids_t, rw_t, og, gw, uw, dw,
    lo_ref, tg_ref, rg_ref, gg, ug, dg,
    pay, gu, dn, gb, hw, hh, crecv, xrecv, zrecv, gstage, grecv, dstage, drecv,
    brecv_s, usend_s, dsend_s, xsend_s, csend_s, wsend_s, wrecv_s,
    gsend_s, grecv_s, qsend_s, qrecv_s,
    c2send_s, c2recv_s, x2send_s, x2recv_s, z2send_s, z2recv_s,
    *sums,
):
    tb, d_all = tok.shape
    dl, hid = gw.shape[1], gw.shape[2]
    top = ids_t.shape[0]
    yb = sums[0] if split else pay
    nz = n // 4
    chunk = 4 * tb
    total = n * tb
    me = lax.axis_index("expert")
    dp = lax.axis_index("dp")
    c = me % 2
    x = (me // 2) % 2
    z = me // 4
    xp = me + 2 - 4 * x
    cp = me + 1 - 2 * c

    def rows(b):
        return pl.ds(pl.multiple_of(b * tb, tb), tb)

    def span(d):
        return pl.ds(pl.multiple_of(d * chunk, chunk), chunk)

    def block(zz, xx, cc):
        return zz * 4 + xx * 2 + cc

    def remote(src, dst, send, recv, **where):
        return pltpu.make_async_remote_copy(
            src_ref=src, dst_ref=dst, send_sem=send, recv_sem=recv,
            device_id=where, device_id_type=MESH,
        )

    barrier = pltpu.get_barrier_semaphore()
    for partner in (xp, cp):
        pl.semaphore_signal(barrier, inc=1, device_id={"expert": partner}, device_id_type=MESH)

    @pl.when(z > 0)
    def _():
        pl.semaphore_signal(barrier, inc=1, device_id={"expert": me - 4}, device_id_type=MESH)

    @pl.when(z < nz - 1)
    def _():
        pl.semaphore_signal(barrier, inc=1, device_id={"expert": me + 4}, device_id_type=MESH)

    for j in range(1, m):
        pl.semaphore_signal(barrier, inc=1, device_id={"dp": (dp + j) % m}, device_id_type=MESH)
    ids = ids_t[...].T
    rw = rw_t[...].T
    lane = lax.broadcasted_iota(jnp.int32, (tb, LANES), 1)
    lane_mod = jnp.where(lane < HALF, lane, lane - HALF)
    dense = jnp.zeros((tb, LANES), F32)
    for k in range(top):
        dense = dense + jnp.where(ids[:, k : k + 1] == lane_mod, rw[:, k : k + 1], 0.0)
    hi = dense.astype(BF16).astype(F32)
    pay[rows(me), 0:d_all] = tok[...]
    pay[rows(me), d_all : 2 * d_all] = og[...]
    pay[rows(me), 2 * d_all :] = jnp.where(lane < HALF, hi, dense - hi).astype(BF16)

    lines = jnp.minimum(z, 1) + jnp.minimum(nz - 1 - z, 1)
    pl.semaphore_wait(barrier, 1 + m + lines)

    my_rows = pl.ds(pl.multiple_of(dp * dl, dl), dl)

    def weight_copies(peer, owner, which=(0, 1, 2)):
        own = pl.ds(pl.multiple_of(owner * dl, dl), dl)
        ends = (
            (gw.at[0], gu.at[own, 0:hid]),
            (uw.at[0], gu.at[own, hid:]),
            (dw.at[0], dn.at[:, own]),
        )
        return [
            remote(*ends[i], wsend_s.at[peer, i], wrecv_s.at[owner, i], dp=peer) for i in which
        ]

    for j in range(1, m):
        for copy in weight_copies((dp + j) % m, dp, (0, 1)):
            copy.start()

    def gather_copy(b, sem, to):
        return remote(pay.at[rows(b)], pay.at[rows(b)], sem, brecv_s.at[b], expert=to)

    def up(zz):
        return gather_copy(block(zz, x, c), usend_s.at[zz], me + 4)

    def down(zz):
        return gather_copy(block(zz, x, c), dsend_s.at[zz], me - 4)

    def across(zz):
        return gather_copy(block(zz, x, c), xsend_s.at[zz], xp)

    def core(zz, xx):
        return gather_copy(block(zz, xx, c), csend_s.at[zz * 2 + xx], cp)

    def arrived(b):
        gather_copy(b, xsend_s.at[0], xp).wait_recv()

    @pl.when(z < nz - 1)
    def _():
        up(z).start()

    @pl.when(z > 0)
    def _():
        down(z).start()

    across(z).start()
    core(z, x).start()
    gu[my_rows, 0:hid] = gw[0]
    gu[my_rows, hid:] = uw[0]
    dn[:, my_rows] = dw[0]

    def partner_blocks(s):
        @pl.when(s == 0)
        def _():
            arrived(block(z, 1 - x, c))
            core(z, 1 - x).start()

        @pl.when((s > 0) & (z - s >= 0))
        def _():
            arrived(block(z - s, 1 - x, c))
            core(z - s, 1 - x).start()

        @pl.when((s > 0) & (z + s < nz))
        def _():
            arrived(block(z + s, 1 - x, c))
            core(z + s, 1 - x).start()

    def gather_step(s, carry):
        @pl.when(z - s >= 0)
        def _():
            arrived(block(z - s, x, c))

            @pl.when(z < nz - 1)
            def _():
                up(z - s).start()

            across(z - s).start()
            core(z - s, x).start()

        @pl.when(z + s < nz)
        def _():
            arrived(block(z + s, x, c))

            @pl.when(z > 0)
            def _():
                down(z + s).start()

            across(z + s).start()
            core(z + s, x).start()

        partner_blocks(s - 1)
        return carry

    lax.fori_loop(1, nz - 1, gather_step, 0)
    for j in range(1, m):
        weight_copies((dp + j) % m, dp, (2,))[0].start()
    gather_step(nz - 1, 0)

    below, above = z, nz - 1 - z
    upward = jnp.minimum(jnp.maximum(above - below, 0), 1)
    excess = jnp.maximum(above - below, below - above)
    paired = jnp.minimum(above, below)

    def order(p):
        inner = jnp.minimum(jnp.maximum(p - excess + 1, 0), 1)
        q = jnp.maximum(p - excess, 0)
        near = z + (paired - q // 2) * (1 - 2 * (q % 2)) * (2 * upward - 1)
        far = upward * (nz - 1 - p) + (1 - upward) * p
        return inner * near + (1 - inner) * far

    wide = lax.broadcasted_iota(jnp.int32, (chunk, LANES), 1)
    mine_hi = wide == me
    mine_lo = wide == me + HALF

    def chunk_weight(r):
        weights = pay[span(r), 2 * d_all :].astype(F32)
        return jnp.sum(jnp.where(mine_hi | mine_lo, weights, 0.0), 1, keepdims=True)

    def act_step(p, carry):
        r = order(nz - 1 - p)
        arrived(block(r, 0, 1 - c))
        arrived(block(r, 1, 1 - c))
        act = jnp.dot(pay[span(r), 0:d_all], gu[...], preferred_element_type=F32)
        gate_act, up_act = act[:, 0:hid], act[:, hid:]
        sig = jax.nn.sigmoid(gate_act)
        silu = gate_act * sig
        hidden = silu * up_act
        hh[span(r), :] = hidden.astype(BF16)
        hw[span(r), :] = (chunk_weight(r) * hidden).astype(BF16)
        gb[span(r), 0:hid] = (up_act * sig * (1.0 + gate_act * (1.0 - sig))).astype(BF16)
        gb[span(r), hid:] = silu.astype(BF16)
        return carry

    for j in range(1, m):
        other = (dp + j) % m
        for copy in weight_copies(other, other, (0, 1)):
            copy.wait_recv()
    lax.fori_loop(0, nz - 1, act_step, 0)
    partner_blocks(nz - 1)
    act_step(nz - 1, 0)

    def gather_sends(zz, carry):
        @pl.when((z < nz - 1) & (zz <= z))
        def _():
            up(zz).wait_send()

        @pl.when((z > 0) & (zz >= z))
        def _():
            down(zz).wait_send()

        across(zz).wait_send()
        core(zz, 0).wait_send()
        core(zz, 1).wait_send()
        return carry

    def back_step(p, carry):
        r = order(p)
        raw = lax.dot_general(pay[span(r), d_all : 2 * d_all], dn[...], LAST, preferred_element_type=F32)
        back = chunk_weight(r) * raw
        route = jnp.sum(hh[span(r), :].astype(F32) * raw, 1, keepdims=True)
        route_hi = route.astype(BF16).astype(F32)
        yb[span(r), 2 * d_all :] = jnp.where(
            mine_hi, route_hi, jnp.where(mine_lo, route - route_hi, 0.0)
        ).astype(BF16)
        gb[span(r), 0:hid] = (back * gb[span(r), 0:hid].astype(F32)).astype(BF16)
        gb[span(r), hid:] = (back * gb[span(r), hid:].astype(F32)).astype(BF16)
        return carry

    piece = min(256, dl)
    pieces = dl // piece
    depth = min(total, 1024)

    def contract(left, right):
        def part(i):
            at = pl.ds(i * depth, depth) if isinstance(i, int) else pl.ds(pl.multiple_of(i * depth, depth), depth)
            return lax.dot_general(left(at), right(at), ROWS, preferred_element_type=F32)

        if total == depth:
            return part(0)
        return lax.fori_loop(1, total // depth, lambda i, acc: acc + part(i), part(0))

    def features(owner, i, shift):
        return pl.ds(pl.multiple_of(shift + owner * dl + i * piece, piece), piece)

    def gate_part(owner, i):
        return contract(lambda at: pay[at, features(owner, i, 0)], lambda at: gb[at, :])

    def down_part(owner):
        mine = pl.ds(pl.multiple_of(d_all + owner * dl, dl), dl)
        return contract(lambda at: hw[at, :], lambda at: pay[at, mine])

    def cut(i):
        return pl.ds(pl.multiple_of(i * piece, piece), piece)

    def gate_copy(peer, owner, i):
        return remote(
            gstage.at[peer, cut(i)], grecv.at[owner, cut(i)],
            gsend_s.at[peer, i], grecv_s.at[owner, i], dp=peer,
        )

    def down_copy(peer, owner):
        return remote(dstage.at[peer], drecv.at[owner], qsend_s.at[peer], qrecv_s.at[owner], dp=peer)

    def down_share(t, carry):
        peer = (dp + 1 + t) % m
        dstage[peer] = down_part(peer).astype(BF16)
        down_copy(peer, dp).start()
        return carry

    def gate_share(t, carry):
        peer = (dp + 1 + t // pieces) % m
        i = t % pieces
        gstage[peer, cut(i)] = gate_part(peer, i).astype(BF16)
        gate_copy(peer, dp, i).start()
        return carry

    def gate_own(i, carry):
        own = gate_part(dp, i)
        gg[0, cut(i), :] = own[:, 0:hid]
        ug[0, cut(i), :] = own[:, hid:]
        return carry

    def core_back(d, xx):
        return remote(
            yb.at[rows(block(d, xx, 1 - c))], crecv.at[d * 2 + xx],
            c2send_s.at[d * 2 + xx], c2recv_s.at[d * 2 + xx], expert=cp,
        )

    def across_back(d):
        return remote(yb.at[rows(block(d, 1 - x, c))], xrecv.at[d], x2send_s.at[d], x2recv_s.at[d], expert=xp)

    def line_back(d, slot, to):
        return remote(yb.at[rows(block(d, x, c))], zrecv.at[slot], z2send_s.at[d], z2recv_s.at[slot], expert=to)

    def add(b, got):
        yb[rows(b), :] = (yb[rows(b), :].astype(F32) + got[...].astype(F32)).astype(BF16)

    def out_step(p, carry):
        d = order(p)
        yb[span(d), 0:d_all] = jnp.dot(hw[span(d), :], dn[...], preferred_element_type=F32).astype(BF16)
        yb[span(d), d_all : 2 * d_all] = lax.dot_general(
            gb[span(d), :], gu[...], LAST, preferred_element_type=F32
        ).astype(BF16)
        core_back(d, 0).start()
        core_back(d, 1).start()
        return carry

    def across_step(p, carry):
        d = order(p)
        core_back(d, 0).wait_recv()
        core_back(d, 1).wait_recv()
        add(block(d, 0, c), crecv.at[d * 2])
        add(block(d, 1, c), crecv.at[d * 2 + 1])
        across_back(d).start()
        return carry

    def take_line(d, slot):
        line_back(d, slot, xp).wait_recv()
        add(block(d, x, c), zrecv.at[slot])

    def line_step(p, carry):
        d = order(p)
        across_back(d).wait_recv()
        add(block(d, x, c), xrecv.at[d])

        @pl.when(d < z)
        def _():
            @pl.when(z < nz - 1)
            def _():
                take_line(d, d)

            line_back(d, d, me - 4).start()

        @pl.when(d > z)
        def _():
            @pl.when(z > 0)
            def _():
                take_line(d, d)

            @pl.when(d > z + 1)
            def _():
                line_back(d, d, me + 4).start()

            @pl.when(d == z + 1)
            def _():
                line_back(d, nz, me + 4).start()

        return carry

    lax.fori_loop(0, m - 1, down_share, 0)
    for j in range(1, m):
        other = (dp + j) % m
        weight_copies(other, other, (2,))[0].wait_recv()

    if split:
        head = 2

        def head_step(p, carry):
            back_step(p, carry)
            return out_step(p, carry)

        def tail_step(p, carry):
            out_step(p, carry)
            return across_step(p - 1, carry)

        lax.fori_loop(0, head, head_step, 0)
        across_step(0, 0)
        lax.fori_loop(head, nz, back_step, 0)
        lax.fori_loop(0, (m - 1) * pieces, gate_share, 0)
        lax.fori_loop(head, nz, tail_step, 0)
        across_step(nz - 1, 0)
        dg[0] = down_part(dp)
        lax.fori_loop(0, pieces, gate_own, 0)
    else:
        lax.fori_loop(0, nz, gather_sends, 0)
        lax.fori_loop(0, nz, back_step, 0)
        lax.fori_loop(0, (m - 1) * pieces, gate_share, 0)
        dg[0] = down_part(dp)
        lax.fori_loop(0, pieces, gate_own, 0)
        lax.fori_loop(0, nz, out_step, 0)
        lax.fori_loop(0, nz, across_step, 0)

    lax.fori_loop(0, nz, line_step, 0)

    @pl.when(z < nz - 1)
    def _():
        take_line(z, z)

    @pl.when(z > 0)
    def _():
        take_line(z, nz)

    lo_ref[...] = yb[rows(me), 0:d_all]
    tg_ref[...] = yb[rows(me), d_all : 2 * d_all]
    route = yb[rows(me), 2 * d_all :].astype(F32)
    slot = lax.broadcasted_iota(jnp.int32, (tb, top), 1)
    picked = jnp.zeros((tb, top), F32)
    for k in range(top):
        value = jnp.sum(jnp.where(ids[:, k : k + 1] == lane_mod, route, 0.0), 1, keepdims=True)
        picked = jnp.where(slot == k, value, picked)
    rg_ref[...] = picked.T

    def share_end(t, carry):
        peer = (dp + 1 + t // pieces) % m
        i = t % pieces
        gate_copy(peer, peer, i).wait()
        gg[0, cut(i), :] += grecv[peer, cut(i), 0:hid].astype(F32)
        ug[0, cut(i), :] += grecv[peer, cut(i), hid:].astype(F32)
        return carry

    def down_end(t, carry):
        peer = (dp + 1 + t) % m
        down_copy(peer, peer).wait()
        dg[0] += drecv[peer].astype(F32)
        return carry

    lax.fori_loop(0, m - 1, down_end, 0)
    lax.fori_loop(0, (m - 1) * pieces, share_end, 0)

    for j in range(1, m):
        for copy in weight_copies((dp + j) % m, dp):
            copy.wait_send()
    if split:
        lax.fori_loop(0, nz, gather_sends, 0)

    def sends_end(d, carry):
        core_back(d, 0).wait_send()
        core_back(d, 1).wait_send()
        across_back(d).wait_send()

        @pl.when(d != z)
        def _():
            line_back(d, d, xp).wait_send()

        return carry

    lax.fori_loop(0, nz, sends_end, 0)


def hand_over(count, *refs):
    ins, outs, held = refs[:count], refs[count : 2 * count], refs[2 * count : 3 * count]
    sems = refs[-1]
    loads = [pltpu.make_async_copy(ins[i], held[i], sems.at[0, i]) for i in range(count)]
    stores = [pltpu.make_async_copy(held[i], outs[i], sems.at[1, i]) for i in range(count)]
    for load in loads:
        load.start()
    for load, store in zip(loads, stores):
        load.wait()
        store.start()
    for store in stores:
        store.wait()


def shards(tokens, expert_ids, route_weight, out_grad, gate_weight, up_weight, down_weight):
    tb, d_all = tokens.shape
    dl, hid = gate_weight.shape[1:]
    n, m = lax.axis_size("expert"), lax.axis_size("dp")
    nz = n // 4
    total = n * tb
    width = 2 * d_all + LANES
    piece = min(256, dl)
    pieces = dl // piece
    dma = pltpu.SemaphoreType.DMA
    vmem = pl.BlockSpec(memory_space=pltpu.VMEM)
    split = total * width * 2 <= 8 * 1024 * 1024
    results = (
        pl.pallas_call(
            functools.partial(kernel, n, m, split),
            out_shape=(
                jax.ShapeDtypeStruct((tb, d_all), BF16),
                jax.ShapeDtypeStruct((tb, d_all), BF16),
                jax.ShapeDtypeStruct(expert_ids.shape[::-1], F32),
                jax.ShapeDtypeStruct((1, dl, hid), F32),
                jax.ShapeDtypeStruct((1, dl, hid), F32),
                jax.ShapeDtypeStruct((1, hid, dl), F32),
            ),
            in_specs=[vmem] * 7,
            out_specs=tuple([vmem] * 6),
            scratch_shapes=[
                pltpu.VMEM((total, width), BF16),
                pltpu.VMEM((d_all, 2 * hid), BF16),
                pltpu.VMEM((hid, d_all), BF16),
                pltpu.VMEM((total, 2 * hid), BF16),
                pltpu.VMEM((total, hid), BF16),
                pltpu.VMEM((total, hid), BF16),
                pltpu.VMEM((2 * nz, tb, width), BF16),
                pltpu.VMEM((nz, tb, width), BF16),
                pltpu.VMEM((nz + 1, tb, width), BF16),
                pltpu.VMEM((m, dl, 2 * hid), BF16),
                pltpu.VMEM((m, dl, 2 * hid), BF16),
                pltpu.VMEM((m, hid, dl), BF16),
                pltpu.VMEM((m, hid, dl), BF16),
                dma((n,)), dma((nz,)), dma((nz,)), dma((nz,)), dma((2 * nz,)), dma((m, 3)), dma((m, 3)),
                dma((m, pieces)), dma((m, pieces)), dma((m,)), dma((m,)),
                dma((2 * nz,)), dma((2 * nz,)), dma((nz,)), dma((nz,)), dma((nz,)), dma((nz + 1,)),
            ]
            + ([pltpu.VMEM((total, width), BF16)] if split else []),
            compiler_params=pltpu.CompilerParams(
                collective_id=0, has_side_effects=True, vmem_limit_bytes=60 * 1024 * 1024
            ),
        )(tokens, expert_ids.T, route_weight.T, out_grad, gate_weight, up_weight, down_weight)
    )
    anywhere = pl.BlockSpec(memory_space=pl.ANY)
    layer_out, token_grad, route_grad, *grads = pl.pallas_call(
        functools.partial(hand_over, len(results)),
        out_shape=tuple(jax.ShapeDtypeStruct(r.shape, r.dtype) for r in results),
        in_specs=[anywhere] * len(results),
        out_specs=tuple([anywhere] * len(results)),
        scratch_shapes=[pltpu.VMEM(r.shape, r.dtype) for r in results] + [dma((2, len(results)))],
        compiler_params=pltpu.CompilerParams(vmem_limit_bytes=60 * 1024 * 1024),
    )(*results)
    return (layer_out, token_grad, route_grad.T, *grads)


def solution(mesh):
    rows = P(("dp", "expert"), None)
    return jax.shard_map(
        shards,
        mesh=mesh,
        in_specs=(rows, rows, rows, rows, P("expert", "dp", None), P("expert", "dp", None), P("expert", None, "dp")),
        out_specs=(rows, rows, rows, P("expert", "dp", None), P("expert", "dp", None), P("expert", None, "dp")),
        check_vma=False,
    )
```

```python
import functools

import jax
import jax.numpy as jnp
from jax import lax
from jax.experimental import pallas as pl
from jax.experimental.pallas import tpu as pltpu
from jax.sharding import PartitionSpec as P

MESH = pl.DeviceIdType.MESH
LANES = 128
HALF = 64
F32 = jnp.float32
BF16 = jnp.bfloat16
LAST = (((1,), (1,)), ((), ()))
ROWS = (((0,), (0,)), ((), ()))


def kernel(
    n, m, split,
    tok, ids_t, rw_t, og, gw, uw, dw,
    lo_ref, tg_ref, rg_ref, gg, ug, dg,
    pay, gu, dn, gb, hw, hh, crecv, xrecv, zrecv, gstage, grecv, dstage, drecv,
    brecv_s, usend_s, dsend_s, xsend_s, csend_s, wsend_s, wrecv_s,
    gsend_s, grecv_s, qsend_s, qrecv_s, local_s,
    c2send_s, c2recv_s, x2send_s, x2recv_s, z2send_s, z2recv_s,
    *sums,
):
    tb, d_all = tok.shape
    dl, hid = gw.shape[1], gw.shape[2]
    top = ids_t.shape[0]
    yb = sums[0] if split else pay
    nz = n // 4
    chunk = 4 * tb
    total = n * tb
    me = lax.axis_index("expert")
    dp = lax.axis_index("dp")
    c = me % 2
    x = (me // 2) % 2
    z = me // 4
    xp = me + 2 - 4 * x
    cp = me + 1 - 2 * c

    def rows(b):
        return pl.ds(pl.multiple_of(b * tb, tb), tb)

    def span(d):
        return pl.ds(pl.multiple_of(d * chunk, chunk), chunk)

    def block(zz, xx, cc):
        return zz * 4 + xx * 2 + cc

    def remote(src, dst, send, recv, **where):
        return pltpu.make_async_remote_copy(
            src_ref=src, dst_ref=dst, send_sem=send, recv_sem=recv,
            device_id=where, device_id_type=MESH,
        )

    barrier = pltpu.get_barrier_semaphore()
    for partner in (xp, cp):
        pl.semaphore_signal(barrier, inc=1, device_id={"expert": partner}, device_id_type=MESH)

    @pl.when(z > 0)
    def _():
        pl.semaphore_signal(barrier, inc=1, device_id={"expert": me - 4}, device_id_type=MESH)

    @pl.when(z < nz - 1)
    def _():
        pl.semaphore_signal(barrier, inc=1, device_id={"expert": me + 4}, device_id_type=MESH)

    for j in range(1, m):
        pl.semaphore_signal(barrier, inc=1, device_id={"dp": (dp + j) % m}, device_id_type=MESH)
    my_rows = pl.ds(pl.multiple_of(dp * dl, dl), dl)
    local = [
        pltpu.make_async_copy(src, dst, local_s.at[i])
        for i, (src, dst) in enumerate(
            (
                (tok, pay.at[rows(me), 0:d_all]),
                (og, pay.at[rows(me), d_all : 2 * d_all]),
                (gw.at[0], gu.at[my_rows, 0:hid]),
                (uw.at[0], gu.at[my_rows, hid:]),
                (dw.at[0], dn.at[:, my_rows]),
            )
        )
    ]
    for copy in local:
        copy.start()
    ids = ids_t[...].T
    rw = rw_t[...].T
    lane = lax.broadcasted_iota(jnp.int32, (tb, LANES), 1)
    lane_mod = jnp.where(lane < HALF, lane, lane - HALF)
    dense = jnp.zeros((tb, LANES), F32)
    for k in range(top):
        dense = dense + jnp.where(ids[:, k : k + 1] == lane_mod, rw[:, k : k + 1], 0.0)
    hi = dense.astype(BF16).astype(F32)
    pay[rows(me), 2 * d_all :] = jnp.where(lane < HALF, hi, dense - hi).astype(BF16)

    lines = jnp.minimum(z, 1) + jnp.minimum(nz - 1 - z, 1)
    pl.semaphore_wait(barrier, 1 + m + lines)

    def weight_copies(peer, owner, which=(0, 1, 2)):
        own = pl.ds(pl.multiple_of(owner * dl, dl), dl)
        ends = (
            (gw.at[0], gu.at[own, 0:hid]),
            (uw.at[0], gu.at[own, hid:]),
            (dw.at[0], dn.at[:, own]),
        )
        return [
            remote(*ends[i], wsend_s.at[peer, i], wrecv_s.at[owner, i], dp=peer) for i in which
        ]

    half = tb // 2

    def gather_copy(b, h, sem, to):
        at = pl.ds(pl.multiple_of(b * tb + h * half, half), half)
        return remote(pay.at[at], pay.at[at], sem, brecv_s.at[b, h], expert=to)

    def up(zz, h):
        return gather_copy(block(zz, x, c), h, usend_s.at[zz, h], me + 4)

    def down(zz, h):
        return gather_copy(block(zz, x, c), h, dsend_s.at[zz, h], me - 4)

    def across(zz, h):
        return gather_copy(block(zz, x, c), h, xsend_s.at[zz, h], xp)

    def core(zz, xx, h):
        return gather_copy(block(zz, xx, c), h, csend_s.at[zz * 2 + xx, h], cp)

    def arrived(b, h):
        gather_copy(b, h, xsend_s.at[0, 0], xp).wait_recv()

    for copy in local[:2]:
        copy.wait()
    for h in range(2):

        @pl.when(z < nz - 1)
        def _():
            up(z, h).start()

        @pl.when(z > 0)
        def _():
            down(z, h).start()

        across(z, h).start()
        core(z, x, h).start()
    for j in range(1, m):
        for copy in weight_copies((dp + j) % m, dp, (0, 1)):
            copy.start()

    def partner_half(zz, h):
        arrived(block(zz, 1 - x, c), h)
        core(zz, 1 - x, h).start()

    def partner_blocks(s):
        for h in range(2):

            @pl.when(s == 0)
            def _():
                partner_half(z, h)

            @pl.when((s > 0) & (z - s >= 0))
            def _():
                partner_half(z - s, h)

            @pl.when((s > 0) & (z + s < nz))
            def _():
                partner_half(z + s, h)

    def gather_step(s, carry):
        for h in range(2):

            @pl.when(z - s >= 0)
            def _():
                arrived(block(z - s, x, c), h)

                @pl.when(z < nz - 1)
                def _():
                    up(z - s, h).start()

                across(z - s, h).start()
                core(z - s, x, h).start()

            @pl.when(z + s < nz)
            def _():
                arrived(block(z + s, x, c), h)

                @pl.when(z > 0)
                def _():
                    down(z + s, h).start()

                across(z + s, h).start()
                core(z + s, x, h).start()

        partner_blocks(s - 1)
        return carry

    lax.fori_loop(1, nz - 1, gather_step, 0)
    for j in range(1, m):
        weight_copies((dp + j) % m, dp, (2,))[0].start()
    gather_step(nz - 1, 0)

    below, above = z, nz - 1 - z
    upward = jnp.minimum(jnp.maximum(above - below, 0), 1)
    excess = jnp.maximum(above - below, below - above)
    paired = jnp.minimum(above, below)

    def order(p):
        inner = jnp.minimum(jnp.maximum(p - excess + 1, 0), 1)
        q = jnp.maximum(p - excess, 0)
        near = z + (paired - q // 2) * (1 - 2 * (q % 2)) * (2 * upward - 1)
        far = upward * (nz - 1 - p) + (1 - upward) * p
        return inner * near + (1 - inner) * far

    wide = lax.broadcasted_iota(jnp.int32, (chunk, LANES), 1)
    mine_hi = wide == me
    mine_lo = wide == me + HALF

    def chunk_weight(r):
        weights = pay[span(r), 2 * d_all :].astype(F32)
        return jnp.sum(jnp.where(mine_hi | mine_lo, weights, 0.0), 1, keepdims=True)

    def act_step(p, carry):
        r = order(nz - 1 - p)
        for h in range(2):
            arrived(block(r, 0, 1 - c), h)
            arrived(block(r, 1, 1 - c), h)
        act = jnp.dot(pay[span(r), 0:d_all], gu[...], preferred_element_type=F32)
        gate_act, up_act = act[:, 0:hid], act[:, hid:]
        sig = jax.nn.sigmoid(gate_act)
        silu = gate_act * sig
        hidden = silu * up_act
        hh[span(r), :] = hidden.astype(BF16)
        hw[span(r), :] = (chunk_weight(r) * hidden).astype(BF16)
        gb[span(r), 0:hid] = (up_act * sig * (1.0 + gate_act * (1.0 - sig))).astype(BF16)
        gb[span(r), hid:] = silu.astype(BF16)
        return carry

    for copy in local[2:]:
        copy.wait()
    for j in range(1, m):
        other = (dp + j) % m
        for copy in weight_copies(other, other, (0, 1)):
            copy.wait_recv()
    lax.fori_loop(0, nz - 1, act_step, 0)
    partner_blocks(nz - 1)
    act_step(nz - 1, 0)

    def gather_sends(zz, carry):
        for h in range(2):

            @pl.when((z < nz - 1) & (zz <= z))
            def _():
                up(zz, h).wait_send()

            @pl.when((z > 0) & (zz >= z))
            def _():
                down(zz, h).wait_send()

            across(zz, h).wait_send()
            core(zz, 0, h).wait_send()
            core(zz, 1, h).wait_send()
        return carry

    def back_step(p, carry):
        r = order(p)
        raw = lax.dot_general(pay[span(r), d_all : 2 * d_all], dn[...], LAST, preferred_element_type=F32)
        back = chunk_weight(r) * raw
        route = jnp.sum(hh[span(r), :].astype(F32) * raw, 1, keepdims=True)
        route_hi = route.astype(BF16).astype(F32)
        yb[span(r), 2 * d_all :] = jnp.where(
            mine_hi, route_hi, jnp.where(mine_lo, route - route_hi, 0.0)
        ).astype(BF16)
        gb[span(r), 0:hid] = (back * gb[span(r), 0:hid].astype(F32)).astype(BF16)
        gb[span(r), hid:] = (back * gb[span(r), hid:].astype(F32)).astype(BF16)
        return carry

    piece = min(256, dl)
    pieces = dl // piece
    depth = min(total, 1024)

    def contract(left, right):
        def part(i):
            at = pl.ds(i * depth, depth) if isinstance(i, int) else pl.ds(pl.multiple_of(i * depth, depth), depth)
            return lax.dot_general(left(at), right(at), ROWS, preferred_element_type=F32)

        if total == depth:
            return part(0)
        return lax.fori_loop(1, total // depth, lambda i, acc: acc + part(i), part(0))

    def features(owner, i, shift):
        return pl.ds(pl.multiple_of(shift + owner * dl + i * piece, piece), piece)

    def gate_part(owner, i):
        return contract(lambda at: pay[at, features(owner, i, 0)], lambda at: gb[at, :])

    def down_part(owner):
        mine = pl.ds(pl.multiple_of(d_all + owner * dl, dl), dl)
        return contract(lambda at: hw[at, :], lambda at: pay[at, mine])

    def cut(i):
        return pl.ds(pl.multiple_of(i * piece, piece), piece)

    def gate_copy(peer, owner, i):
        return remote(
            gstage.at[peer, cut(i)], grecv.at[owner, cut(i)],
            gsend_s.at[peer, i], grecv_s.at[owner, i], dp=peer,
        )

    def down_copy(peer, owner):
        return remote(dstage.at[peer], drecv.at[owner], qsend_s.at[peer], qrecv_s.at[owner], dp=peer)

    def down_share(t, carry):
        peer = (dp + 1 + t) % m
        dstage[peer] = down_part(peer).astype(BF16)
        down_copy(peer, dp).start()
        return carry

    def gate_share(t, carry):
        peer = (dp + 1 + t // pieces) % m
        i = t % pieces
        gstage[peer, cut(i)] = gate_part(peer, i).astype(BF16)
        gate_copy(peer, dp, i).start()
        return carry

    def gate_own(i, carry):
        own = gate_part(dp, i)
        gg[0, cut(i), :] = own[:, 0:hid]
        ug[0, cut(i), :] = own[:, hid:]
        return carry

    def core_back(d, xx):
        return remote(
            yb.at[rows(block(d, xx, 1 - c))], crecv.at[d * 2 + xx],
            c2send_s.at[d * 2 + xx], c2recv_s.at[d * 2 + xx], expert=cp,
        )

    def across_back(d):
        return remote(yb.at[rows(block(d, 1 - x, c))], xrecv.at[d], x2send_s.at[d], x2recv_s.at[d], expert=xp)

    def line_back(d, slot, to):
        return remote(yb.at[rows(block(d, x, c))], zrecv.at[slot], z2send_s.at[d], z2recv_s.at[slot], expert=to)

    def add(b, got):
        yb[rows(b), :] = (yb[rows(b), :].astype(F32) + got[...].astype(F32)).astype(BF16)

    def out_step(p, carry):
        d = order(p)
        yb[span(d), 0:d_all] = jnp.dot(hw[span(d), :], dn[...], preferred_element_type=F32).astype(BF16)
        yb[span(d), d_all : 2 * d_all] = lax.dot_general(
            gb[span(d), :], gu[...], LAST, preferred_element_type=F32
        ).astype(BF16)
        core_back(d, 0).start()
        core_back(d, 1).start()
        return carry

    def across_step(p, carry):
        d = order(p)
        core_back(d, 0).wait_recv()
        core_back(d, 1).wait_recv()
        add(block(d, 0, c), crecv.at[d * 2])
        add(block(d, 1, c), crecv.at[d * 2 + 1])
        across_back(d).start()
        return carry

    def take_line(d, slot):
        line_back(d, slot, xp).wait_recv()
        add(block(d, x, c), zrecv.at[slot])

    def line_step(p, carry):
        d = order(p)
        across_back(d).wait_recv()
        add(block(d, x, c), xrecv.at[d])

        @pl.when(d < z)
        def _():
            @pl.when(z < nz - 1)
            def _():
                take_line(d, d)

            line_back(d, d, me - 4).start()

        @pl.when(d > z)
        def _():
            @pl.when(z > 0)
            def _():
                take_line(d, d)

            @pl.when(d > z + 1)
            def _():
                line_back(d, d, me + 4).start()

            @pl.when(d == z + 1)
            def _():
                line_back(d, nz, me + 4).start()

        return carry

    for j in range(1, m):
        other = (dp + j) % m
        weight_copies(other, other, (2,))[0].wait_recv()

    if split:

        def tail_step(p, carry):
            out_step(p, carry)
            return across_step(p - 1, carry)

        back_step(0, 0)
        out_step(0, 0)
        lax.fori_loop(0, m - 1, down_share, 0)
        across_step(0, 0)
        lax.fori_loop(1, nz, back_step, 0)
        out_step(1, 0)
        lax.fori_loop(0, (m - 1) * pieces, gate_share, 0)
        lax.fori_loop(2, nz, tail_step, 0)
        across_step(nz - 1, 0)
        dg[0] = down_part(dp)
        lax.fori_loop(0, pieces, gate_own, 0)
    else:
        lax.fori_loop(0, m - 1, down_share, 0)
        lax.fori_loop(0, nz, gather_sends, 0)
        lax.fori_loop(0, nz, back_step, 0)
        lax.fori_loop(0, (m - 1) * pieces, gate_share, 0)
        dg[0] = down_part(dp)
        lax.fori_loop(0, pieces, gate_own, 0)
        lax.fori_loop(0, nz, out_step, 0)
        lax.fori_loop(0, nz, across_step, 0)

    lax.fori_loop(0, nz, line_step, 0)

    @pl.when(z < nz - 1)
    def _():
        take_line(z, z)

    @pl.when(z > 0)
    def _():
        take_line(z, nz)

    lo_ref[...] = yb[rows(me), 0:d_all]
    tg_ref[...] = yb[rows(me), d_all : 2 * d_all]
    route = yb[rows(me), 2 * d_all :].astype(F32)
    slot = lax.broadcasted_iota(jnp.int32, (tb, top), 1)
    picked = jnp.zeros((tb, top), F32)
    for k in range(top):
        value = jnp.sum(jnp.where(ids[:, k : k + 1] == lane_mod, route, 0.0), 1, keepdims=True)
        picked = jnp.where(slot == k, value, picked)
    rg_ref[...] = picked.T

    def share_end(t, carry):
        peer = (dp + 1 + t // pieces) % m
        i = t % pieces
        gate_copy(peer, peer, i).wait()
        gg[0, cut(i), :] += grecv[peer, cut(i), 0:hid].astype(F32)
        ug[0, cut(i), :] += grecv[peer, cut(i), hid:].astype(F32)
        return carry

    def down_end(t, carry):
        peer = (dp + 1 + t) % m
        down_copy(peer, peer).wait()
        dg[0] += drecv[peer].astype(F32)
        return carry

    lax.fori_loop(0, m - 1, down_end, 0)
    lax.fori_loop(0, (m - 1) * pieces, share_end, 0)

    for j in range(1, m):
        for copy in weight_copies((dp + j) % m, dp):
            copy.wait_send()
    if split:
        lax.fori_loop(0, nz, gather_sends, 0)

    def sends_end(d, carry):
        core_back(d, 0).wait_send()
        core_back(d, 1).wait_send()
        across_back(d).wait_send()

        @pl.when(d != z)
        def _():
            line_back(d, d, xp).wait_send()

        return carry

    lax.fori_loop(0, nz, sends_end, 0)


def hand_over(count, *refs):
    ins, outs, held = refs[:count], refs[count : 2 * count], refs[2 * count : 3 * count]
    sems = refs[-1]
    loads = [pltpu.make_async_copy(ins[i], held[i], sems.at[0, i]) for i in range(count)]
    stores = [pltpu.make_async_copy(held[i], outs[i], sems.at[1, i]) for i in range(count)]
    for load in loads:
        load.start()
    for load, store in zip(loads, stores):
        load.wait()
        store.start()
    for store in stores:
        store.wait()


def shards(tokens, expert_ids, route_weight, out_grad, gate_weight, up_weight, down_weight):
    tb, d_all = tokens.shape
    dl, hid = gate_weight.shape[1:]
    n, m = lax.axis_size("expert"), lax.axis_size("dp")
    nz = n // 4
    total = n * tb
    width = 2 * d_all + LANES
    piece = min(256, dl)
    pieces = dl // piece
    dma = pltpu.SemaphoreType.DMA
    vmem = pl.BlockSpec(memory_space=pltpu.VMEM)
    anywhere = pl.BlockSpec(memory_space=pl.ANY)
    split = total * width * 2 <= 8 * 1024 * 1024
    results = (
        pl.pallas_call(
            functools.partial(kernel, n, m, split),
            out_shape=(
                jax.ShapeDtypeStruct((tb, d_all), BF16),
                jax.ShapeDtypeStruct((tb, d_all), BF16),
                jax.ShapeDtypeStruct(expert_ids.shape[::-1], F32),
                jax.ShapeDtypeStruct((1, dl, hid), F32),
                jax.ShapeDtypeStruct((1, dl, hid), F32),
                jax.ShapeDtypeStruct((1, hid, dl), F32),
            ),
            in_specs=[anywhere, vmem, vmem] + [anywhere] * 4,
            out_specs=tuple([vmem] * 6),
            scratch_shapes=[
                pltpu.VMEM((total, width), BF16),
                pltpu.VMEM((d_all, 2 * hid), BF16),
                pltpu.VMEM((hid, d_all), BF16),
                pltpu.VMEM((total, 2 * hid), BF16),
                pltpu.VMEM((total, hid), BF16),
                pltpu.VMEM((total, hid), BF16),
                pltpu.VMEM((2 * nz, tb, width), BF16),
                pltpu.VMEM((nz, tb, width), BF16),
                pltpu.VMEM((nz + 1, tb, width), BF16),
                pltpu.VMEM((m, dl, 2 * hid), BF16),
                pltpu.VMEM((m, dl, 2 * hid), BF16),
                pltpu.VMEM((m, hid, dl), BF16),
                pltpu.VMEM((m, hid, dl), BF16),
                dma((n, 2)), dma((nz, 2)), dma((nz, 2)), dma((nz, 2)), dma((2 * nz, 2)), dma((m, 3)), dma((m, 3)),
                dma((m, pieces)), dma((m, pieces)), dma((m,)), dma((m,)), dma((5,)),
                dma((2 * nz,)), dma((2 * nz,)), dma((nz,)), dma((nz,)), dma((nz,)), dma((nz + 1,)),
            ]
            + ([pltpu.VMEM((total, width), BF16)] if split else []),
            compiler_params=pltpu.CompilerParams(
                collective_id=0, has_side_effects=True, vmem_limit_bytes=60 * 1024 * 1024
            ),
        )(tokens, expert_ids.T, route_weight.T, out_grad, gate_weight, up_weight, down_weight)
    )
    layer_out, token_grad, route_grad, *grads = pl.pallas_call(
        functools.partial(hand_over, len(results)),
        out_shape=tuple(jax.ShapeDtypeStruct(r.shape, r.dtype) for r in results),
        in_specs=[anywhere] * len(results),
        out_specs=tuple([anywhere] * len(results)),
        scratch_shapes=[pltpu.VMEM(r.shape, r.dtype) for r in results] + [dma((2, len(results)))],
        compiler_params=pltpu.CompilerParams(vmem_limit_bytes=60 * 1024 * 1024),
    )(*results)
    return (layer_out, token_grad, route_grad.T, *grads)


def solution(mesh):
    rows = P(("dp", "expert"), None)
    return jax.shard_map(
        shards,
        mesh=mesh,
        in_specs=(rows, rows, rows, rows, P("expert", "dp", None), P("expert", "dp", None), P("expert", None, "dp")),
        out_specs=(rows, rows, rows, P("expert", "dp", None), P("expert", "dp", None), P("expert", None, "dp")),
        check_vma=False,
    )
```

```python
import functools

import jax
import jax.numpy as jnp
from jax import lax
from jax.experimental import pallas as pl
from jax.experimental.pallas import tpu as pltpu
from jax.sharding import PartitionSpec as P

MESH = pl.DeviceIdType.MESH
LANES = 128
HALF = 64
F32 = jnp.float32
BF16 = jnp.bfloat16
LAST = (((1,), (1,)), ((), ()))
ROWS = (((0,), (0,)), ((), ()))


def kernel(
    n, m, split,
    tok, ids_t, rw_t, og, gw, uw, dw,
    lo_ref, tg_ref, rg_ref, gg, ug, dg,
    pay, gu, dn, gb, hw, hh, crecv, xrecv, zrecv, gstage, grecv, dstage, drecv,
    brecv_s, usend_s, dsend_s, xsend_s, csend_s, wsend_s, wrecv_s,
    gsend_s, grecv_s, qsend_s, qrecv_s, local_s,
    c2send_s, c2recv_s, x2send_s, x2recv_s, z2send_s, z2recv_s,
    *sums,
):
    tb, d_all = tok.shape
    dl, hid = gw.shape[1], gw.shape[2]
    top = ids_t.shape[0]
    yb = sums[0] if split else pay
    nz = n // 4
    chunk = 4 * tb
    total = n * tb
    me = lax.axis_index("expert")
    dp = lax.axis_index("dp")
    c = me % 2
    x = (me // 2) % 2
    z = me // 4
    xp = me + 2 - 4 * x
    cp = me + 1 - 2 * c

    def rows(b):
        return pl.ds(pl.multiple_of(b * tb, tb), tb)

    def span(d):
        return pl.ds(pl.multiple_of(d * chunk, chunk), chunk)

    def block(zz, xx, cc):
        return zz * 4 + xx * 2 + cc

    def remote(src, dst, send, recv, **where):
        return pltpu.make_async_remote_copy(
            src_ref=src, dst_ref=dst, send_sem=send, recv_sem=recv,
            device_id=where, device_id_type=MESH,
        )

    barrier = pltpu.get_barrier_semaphore()
    for partner in (xp, cp):
        pl.semaphore_signal(barrier, inc=1, device_id={"expert": partner}, device_id_type=MESH)

    @pl.when(z > 0)
    def _():
        pl.semaphore_signal(barrier, inc=1, device_id={"expert": me - 4}, device_id_type=MESH)

    @pl.when(z < nz - 1)
    def _():
        pl.semaphore_signal(barrier, inc=1, device_id={"expert": me + 4}, device_id_type=MESH)

    for j in range(1, m):
        pl.semaphore_signal(barrier, inc=1, device_id={"dp": (dp + j) % m}, device_id_type=MESH)
    my_rows = pl.ds(pl.multiple_of(dp * dl, dl), dl)
    local = [
        pltpu.make_async_copy(src, dst, local_s.at[i])
        for i, (src, dst) in enumerate(
            (
                (tok, pay.at[rows(me), 0:d_all]),
                (og, pay.at[rows(me), d_all : 2 * d_all]),
                (gw.at[0], gu.at[my_rows, 0:hid]),
                (uw.at[0], gu.at[my_rows, hid:]),
                (dw.at[0], dn.at[:, my_rows]),
            )
        )
    ]
    for copy in local:
        copy.start()
    ids = ids_t[...].T
    rw = rw_t[...].T
    lane = lax.broadcasted_iota(jnp.int32, (tb, LANES), 1)
    lane_mod = jnp.where(lane < HALF, lane, lane - HALF)
    dense = jnp.zeros((tb, LANES), F32)
    for k in range(top):
        dense = dense + jnp.where(ids[:, k : k + 1] == lane_mod, rw[:, k : k + 1], 0.0)
    hi = dense.astype(BF16).astype(F32)
    pay[rows(me), 2 * d_all :] = jnp.where(lane < HALF, hi, dense - hi).astype(BF16)

    lines = jnp.minimum(z, 1) + jnp.minimum(nz - 1 - z, 1)
    pl.semaphore_wait(barrier, 1 + m + lines)

    def weight_copies(peer, owner, which=(0, 1, 2)):
        own = pl.ds(pl.multiple_of(owner * dl, dl), dl)
        ends = (
            (gw.at[0], gu.at[own, 0:hid]),
            (uw.at[0], gu.at[own, hid:]),
            (dw.at[0], dn.at[:, own]),
        )
        return [
            remote(*ends[i], wsend_s.at[peer, i], wrecv_s.at[owner, i], dp=peer) for i in which
        ]

    half = tb // 2

    def gather_copy(b, h, sem, to):
        at = pl.ds(pl.multiple_of(b * tb + h * half, half), half)
        return remote(pay.at[at], pay.at[at], sem, brecv_s.at[b, h], expert=to)

    def up(zz, h):
        return gather_copy(block(zz, x, c), h, usend_s.at[zz, h], me + 4)

    def down(zz, h):
        return gather_copy(block(zz, x, c), h, dsend_s.at[zz, h], me - 4)

    def across(zz, h):
        return gather_copy(block(zz, x, c), h, xsend_s.at[zz, h], xp)

    def core(zz, xx, h):
        return gather_copy(block(zz, xx, c), h, csend_s.at[zz * 2 + xx, h], cp)

    def arrived(b, h):
        gather_copy(b, h, xsend_s.at[0, 0], xp).wait_recv()

    for copy in local[:2]:
        copy.wait()
    for h in range(2):

        @pl.when(z < nz - 1)
        def _():
            up(z, h).start()

        @pl.when(z > 0)
        def _():
            down(z, h).start()

        across(z, h).start()
        core(z, x, h).start()
    for j in range(1, m):
        for copy in weight_copies((dp + j) % m, dp, (0, 1)):
            copy.start()

    def partner_half(zz, h):
        arrived(block(zz, 1 - x, c), h)
        core(zz, 1 - x, h).start()

    def partner_blocks(s):
        for h in range(2):

            @pl.when(s == 0)
            def _():
                partner_half(z, h)

            @pl.when((s > 0) & (z - s >= 0))
            def _():
                partner_half(z - s, h)

            @pl.when((s > 0) & (z + s < nz))
            def _():
                partner_half(z + s, h)

    def gather_step(s, carry):
        for h in range(2):

            @pl.when(z - s >= 0)
            def _():
                arrived(block(z - s, x, c), h)

                @pl.when(z < nz - 1)
                def _():
                    up(z - s, h).start()

                across(z - s, h).start()
                core(z - s, x, h).start()

            @pl.when(z + s < nz)
            def _():
                arrived(block(z + s, x, c), h)

                @pl.when(z > 0)
                def _():
                    down(z + s, h).start()

                across(z + s, h).start()
                core(z + s, x, h).start()

        partner_blocks(s - 1)
        return carry

    lax.fori_loop(1, nz - 1, gather_step, 0)
    for j in range(1, m):
        weight_copies((dp + j) % m, dp, (2,))[0].start()
    gather_step(nz - 1, 0)

    below, above = z, nz - 1 - z
    upward = jnp.minimum(jnp.maximum(above - below, 0), 1)
    excess = jnp.maximum(above - below, below - above)
    paired = jnp.minimum(above, below)

    def order(p):
        inner = jnp.minimum(jnp.maximum(p - excess + 1, 0), 1)
        q = jnp.maximum(p - excess, 0)
        near = z + (paired - q // 2) * (1 - 2 * (q % 2)) * (2 * upward - 1)
        far = upward * (nz - 1 - p) + (1 - upward) * p
        return inner * near + (1 - inner) * far

    wide = lax.broadcasted_iota(jnp.int32, (chunk, LANES), 1)
    mine_hi = wide == me
    mine_lo = wide == me + HALF

    def chunk_weight(r):
        weights = pay[span(r), 2 * d_all :].astype(F32)
        return jnp.sum(jnp.where(mine_hi | mine_lo, weights, 0.0), 1, keepdims=True)

    def act_step(p, carry):
        r = order(nz - 1 - p)
        for h in range(2):
            arrived(block(r, 0, 1 - c), h)
            arrived(block(r, 1, 1 - c), h)
        act = jnp.dot(pay[span(r), 0:d_all], gu[...], preferred_element_type=F32)
        gate_act, up_act = act[:, 0:hid], act[:, hid:]
        sig = jax.nn.sigmoid(gate_act)
        silu = gate_act * sig
        hidden = silu * up_act
        hh[span(r), :] = hidden.astype(BF16)
        hw[span(r), :] = (chunk_weight(r) * hidden).astype(BF16)
        gb[span(r), 0:hid] = (up_act * sig * (1.0 + gate_act * (1.0 - sig))).astype(BF16)
        gb[span(r), hid:] = silu.astype(BF16)
        return carry

    for copy in local[2:]:
        copy.wait()
    for j in range(1, m):
        other = (dp + j) % m
        for copy in weight_copies(other, other, (0, 1)):
            copy.wait_recv()
    lax.fori_loop(0, nz - 1, act_step, 0)
    partner_blocks(nz - 1)
    act_step(nz - 1, 0)

    def gather_sends(zz, carry):
        for h in range(2):

            @pl.when((z < nz - 1) & (zz <= z))
            def _():
                up(zz, h).wait_send()

            @pl.when((z > 0) & (zz >= z))
            def _():
                down(zz, h).wait_send()

            across(zz, h).wait_send()
            core(zz, 0, h).wait_send()
            core(zz, 1, h).wait_send()
        return carry

    def back_step(p, carry):
        r = order(p)
        raw = lax.dot_general(pay[span(r), d_all : 2 * d_all], dn[...], LAST, preferred_element_type=F32)
        back = chunk_weight(r) * raw
        route = jnp.sum(hh[span(r), :].astype(F32) * raw, 1, keepdims=True)
        route_hi = route.astype(BF16).astype(F32)
        yb[span(r), 2 * d_all :] = jnp.where(
            mine_hi, route_hi, jnp.where(mine_lo, route - route_hi, 0.0)
        ).astype(BF16)
        gb[span(r), 0:hid] = (back * gb[span(r), 0:hid].astype(F32)).astype(BF16)
        gb[span(r), hid:] = (back * gb[span(r), hid:].astype(F32)).astype(BF16)
        return carry

    piece = min(256, dl)
    pieces = dl // piece
    depth = min(total, 1024)

    def contract(left, right):
        def part(i):
            at = pl.ds(i * depth, depth) if isinstance(i, int) else pl.ds(pl.multiple_of(i * depth, depth), depth)
            return lax.dot_general(left(at), right(at), ROWS, preferred_element_type=F32)

        if total == depth:
            return part(0)
        return lax.fori_loop(1, total // depth, lambda i, acc: acc + part(i), part(0))

    def features(owner, i, shift):
        return pl.ds(pl.multiple_of(shift + owner * dl + i * piece, piece), piece)

    def gate_part(owner, i):
        return contract(lambda at: pay[at, features(owner, i, 0)], lambda at: gb[at, :])

    def down_part(owner):
        mine = pl.ds(pl.multiple_of(d_all + owner * dl, dl), dl)
        return contract(lambda at: hw[at, :], lambda at: pay[at, mine])

    def cut(i):
        return pl.ds(pl.multiple_of(i * piece, piece), piece)

    def gate_copy(peer, owner, i):
        return remote(
            gstage.at[peer, cut(i)], grecv.at[owner, cut(i)],
            gsend_s.at[peer, i], grecv_s.at[owner, i], dp=peer,
        )

    def down_copy(peer, owner):
        return remote(dstage.at[peer], drecv.at[owner], qsend_s.at[peer], qrecv_s.at[owner], dp=peer)

    def down_share(t, carry):
        peer = (dp + 1 + t) % m
        dstage[peer] = down_part(peer).astype(BF16)
        down_copy(peer, dp).start()
        return carry

    def gate_share(t, carry):
        peer = (dp + 1 + t // pieces) % m
        i = t % pieces
        gstage[peer, cut(i)] = gate_part(peer, i).astype(BF16)
        gate_copy(peer, dp, i).start()
        return carry

    def gate_own(i, carry):
        own = gate_part(dp, i)
        gg[0, cut(i), :] = own[:, 0:hid]
        ug[0, cut(i), :] = own[:, hid:]
        return carry

    def core_back(d, xx):
        return remote(
            yb.at[rows(block(d, xx, 1 - c))], crecv.at[d * 2 + xx],
            c2send_s.at[d * 2 + xx], c2recv_s.at[d * 2 + xx], expert=cp,
        )

    def across_back(d):
        return remote(yb.at[rows(block(d, 1 - x, c))], xrecv.at[d], x2send_s.at[d], x2recv_s.at[d], expert=xp)

    def half_rows(b, h):
        return pl.ds(pl.multiple_of(b * tb + h * half, half), half)

    def line_back(d, slot, h, to):
        return remote(
            yb.at[half_rows(block(d, x, c), h)], zrecv.at[slot, pl.ds(h * half, half)],
            z2send_s.at[d, h], z2recv_s.at[slot, h], expert=to,
        )

    def add(b, got):
        yb[rows(b), :] = (yb[rows(b), :].astype(F32) + got[...].astype(F32)).astype(BF16)

    def out_step(p, carry):
        d = order(p)
        yb[span(d), 0:d_all] = jnp.dot(hw[span(d), :], dn[...], preferred_element_type=F32).astype(BF16)
        yb[span(d), d_all : 2 * d_all] = lax.dot_general(
            gb[span(d), :], gu[...], LAST, preferred_element_type=F32
        ).astype(BF16)
        core_back(d, 0).start()
        core_back(d, 1).start()
        return carry

    def across_step(p, carry):
        d = order(p)
        core_back(d, 0).wait_recv()
        core_back(d, 1).wait_recv()
        add(block(d, 0, c), crecv.at[d * 2])
        add(block(d, 1, c), crecv.at[d * 2 + 1])
        across_back(d).start()
        return carry

    def take_line(d, slot, h):
        line_back(d, slot, h, xp).wait_recv()
        at = half_rows(block(d, x, c), h)
        got = zrecv[slot, pl.ds(h * half, half), :]
        yb[at, :] = (yb[at, :].astype(F32) + got.astype(F32)).astype(BF16)

    def line_step(p, carry):
        d = order(p)
        across_back(d).wait_recv()
        add(block(d, x, c), xrecv.at[d])
        for h in range(2):

            @pl.when(d < z)
            def _():
                @pl.when(z < nz - 1)
                def _():
                    take_line(d, d, h)

                line_back(d, d, h, me - 4).start()

            @pl.when(d > z)
            def _():
                @pl.when(z > 0)
                def _():
                    take_line(d, d, h)

                @pl.when(d > z + 1)
                def _():
                    line_back(d, d, h, me + 4).start()

                @pl.when(d == z + 1)
                def _():
                    line_back(d, nz, h, me + 4).start()

        return carry

    for j in range(1, m):
        other = (dp + j) % m
        weight_copies(other, other, (2,))[0].wait_recv()

    if split:

        def more_step(p, carry):
            out_step(p, carry)
            return across_step(p, carry)

        back_step(0, 0)
        out_step(0, 0)
        lax.fori_loop(0, m - 1, down_share, 0)
        across_step(0, 0)
        back_step(1, 0)
        more_step(1, 0)
        lax.fori_loop(2, nz, back_step, 0)
        lax.fori_loop(0, (m - 1) * pieces, gate_share, 0)
        lax.fori_loop(2, nz, more_step, 0)
        line_step(0, 0)
        dg[0] = down_part(dp)
        line_step(1, 0)
        lax.fori_loop(0, pieces, gate_own, 0)
        lax.fori_loop(2, nz, line_step, 0)
    else:
        lax.fori_loop(0, m - 1, down_share, 0)
        lax.fori_loop(0, nz, gather_sends, 0)
        lax.fori_loop(0, nz, back_step, 0)
        lax.fori_loop(0, (m - 1) * pieces, gate_share, 0)
        dg[0] = down_part(dp)
        lax.fori_loop(0, pieces, gate_own, 0)
        lax.fori_loop(0, nz, out_step, 0)
        lax.fori_loop(0, nz, across_step, 0)
        lax.fori_loop(0, nz, line_step, 0)

    @pl.when(z < nz - 1)
    def _():
        take_line(z, z, 0)
        take_line(z, z, 1)

    @pl.when(z > 0)
    def _():
        take_line(z, nz, 0)
        take_line(z, nz, 1)

    lo_ref[...] = yb[rows(me), 0:d_all]
    tg_ref[...] = yb[rows(me), d_all : 2 * d_all]
    route = yb[rows(me), 2 * d_all :].astype(F32)
    slot = lax.broadcasted_iota(jnp.int32, (tb, top), 1)
    picked = jnp.zeros((tb, top), F32)
    for k in range(top):
        value = jnp.sum(jnp.where(ids[:, k : k + 1] == lane_mod, route, 0.0), 1, keepdims=True)
        picked = jnp.where(slot == k, value, picked)
    rg_ref[...] = picked.T

    def share_end(t, carry):
        peer = (dp + 1 + t // pieces) % m
        i = t % pieces
        gate_copy(peer, peer, i).wait()
        gg[0, cut(i), :] += grecv[peer, cut(i), 0:hid].astype(F32)
        ug[0, cut(i), :] += grecv[peer, cut(i), hid:].astype(F32)
        return carry

    def down_end(t, carry):
        peer = (dp + 1 + t) % m
        down_copy(peer, peer).wait()
        dg[0] += drecv[peer].astype(F32)
        return carry

    lax.fori_loop(0, m - 1, down_end, 0)
    lax.fori_loop(0, (m - 1) * pieces, share_end, 0)

    for j in range(1, m):
        for copy in weight_copies((dp + j) % m, dp):
            copy.wait_send()
    if split:
        lax.fori_loop(0, nz, gather_sends, 0)

    def sends_end(d, carry):
        core_back(d, 0).wait_send()
        core_back(d, 1).wait_send()
        across_back(d).wait_send()

        @pl.when(d != z)
        def _():
            line_back(d, d, 0, xp).wait_send()
            line_back(d, d, 1, xp).wait_send()

        return carry

    lax.fori_loop(0, nz, sends_end, 0)


def hand_over(count, *refs):
    ins, outs, held = refs[:count], refs[count : 2 * count], refs[2 * count : 3 * count]
    sems = refs[-1]
    loads = [pltpu.make_async_copy(ins[i], held[i], sems.at[0, i]) for i in range(count)]
    stores = [pltpu.make_async_copy(held[i], outs[i], sems.at[1, i]) for i in range(count)]
    for load in loads:
        load.start()
    for load, store in zip(loads, stores):
        load.wait()
        store.start()
    for store in stores:
        store.wait()


def shards(tokens, expert_ids, route_weight, out_grad, gate_weight, up_weight, down_weight):
    tb, d_all = tokens.shape
    dl, hid = gate_weight.shape[1:]
    n, m = lax.axis_size("expert"), lax.axis_size("dp")
    nz = n // 4
    total = n * tb
    width = 2 * d_all + LANES
    piece = min(256, dl)
    pieces = dl // piece
    dma = pltpu.SemaphoreType.DMA
    vmem = pl.BlockSpec(memory_space=pltpu.VMEM)
    anywhere = pl.BlockSpec(memory_space=pl.ANY)
    split = total * width * 2 <= 8 * 1024 * 1024
    results = (
        pl.pallas_call(
            functools.partial(kernel, n, m, split),
            out_shape=(
                jax.ShapeDtypeStruct((tb, d_all), BF16),
                jax.ShapeDtypeStruct((tb, d_all), BF16),
                jax.ShapeDtypeStruct(expert_ids.shape[::-1], F32),
                jax.ShapeDtypeStruct((1, dl, hid), F32),
                jax.ShapeDtypeStruct((1, dl, hid), F32),
                jax.ShapeDtypeStruct((1, hid, dl), F32),
            ),
            in_specs=[anywhere, vmem, vmem] + [anywhere] * 4,
            out_specs=tuple([vmem] * 6),
            scratch_shapes=[
                pltpu.VMEM((total, width), BF16),
                pltpu.VMEM((d_all, 2 * hid), BF16),
                pltpu.VMEM((hid, d_all), BF16),
                pltpu.VMEM((total, 2 * hid), BF16),
                pltpu.VMEM((total, hid), BF16),
                pltpu.VMEM((total, hid), BF16),
                pltpu.VMEM((2 * nz, tb, width), BF16),
                pltpu.VMEM((nz, tb, width), BF16),
                pltpu.VMEM((nz + 1, tb, width), BF16),
                pltpu.VMEM((m, dl, 2 * hid), BF16),
                pltpu.VMEM((m, dl, 2 * hid), BF16),
                pltpu.VMEM((m, hid, dl), BF16),
                pltpu.VMEM((m, hid, dl), BF16),
                dma((n, 2)), dma((nz, 2)), dma((nz, 2)), dma((nz, 2)), dma((2 * nz, 2)), dma((m, 3)), dma((m, 3)),
                dma((m, pieces)), dma((m, pieces)), dma((m,)), dma((m,)), dma((5,)),
                dma((2 * nz,)), dma((2 * nz,)), dma((nz,)), dma((nz,)), dma((nz, 2)), dma((nz + 1, 2)),
            ]
            + ([pltpu.VMEM((total, width), BF16)] if split else []),
            compiler_params=pltpu.CompilerParams(
                collective_id=0, has_side_effects=True, vmem_limit_bytes=60 * 1024 * 1024
            ),
        )(tokens, expert_ids.T, route_weight.T, out_grad, gate_weight, up_weight, down_weight)
    )
    layer_out, token_grad, route_grad, *grads = pl.pallas_call(
        functools.partial(hand_over, len(results)),
        out_shape=tuple(jax.ShapeDtypeStruct(r.shape, r.dtype) for r in results),
        in_specs=[anywhere] * len(results),
        out_specs=tuple([anywhere] * len(results)),
        scratch_shapes=[pltpu.VMEM(r.shape, r.dtype) for r in results] + [dma((2, len(results)))],
        compiler_params=pltpu.CompilerParams(vmem_limit_bytes=60 * 1024 * 1024),
    )(*results)
    return (layer_out, token_grad, route_grad.T, *grads)


def solution(mesh):
    rows = P(("dp", "expert"), None)
    return jax.shard_map(
        shards,
        mesh=mesh,
        in_specs=(rows, rows, rows, rows, P("expert", "dp", None), P("expert", "dp", None), P("expert", None, "dp")),
        out_specs=(rows, rows, rows, P("expert", "dp", None), P("expert", "dp", None), P("expert", None, "dp")),
        check_vma=False,
    )
```

```python
import functools

import jax
import jax.numpy as jnp
from jax import lax
from jax.experimental import pallas as pl
from jax.experimental.pallas import tpu as pltpu
from jax.sharding import PartitionSpec as P

MESH = pl.DeviceIdType.MESH
LANES = 128
HALF = 64
F32 = jnp.float32
BF16 = jnp.bfloat16
LAST = (((1,), (1,)), ((), ()))
ROWS = (((0,), (0,)), ((), ()))


def kernel(
    n, m, split,
    tok, ids_t, rw_t, og, gw, uw, dw,
    lo_ref, tg_ref, rg_ref, gg, ug, dg,
    pay, gu, dn, gb, hw, hh, crecv, xrecv, zrecv, gstage, grecv, dstage, drecv,
    brecv_s, usend_s, dsend_s, xsend_s, csend_s, wsend_s, wrecv_s,
    gsend_s, grecv_s, qsend_s, qrecv_s, local_s,
    c2send_s, c2recv_s, x2send_s, x2recv_s, z2send_s, z2recv_s,
    *sums,
):
    tb, d_all = tok.shape
    dl, hid = gw.shape[1], gw.shape[2]
    top = ids_t.shape[0]
    yb = sums[0] if split else pay
    if split:
        gu_t, dn_t, x_t, hw_t = sums[1:]
    nz = n // 4
    chunk = 4 * tb
    total = n * tb
    me = lax.axis_index("expert")
    dp = lax.axis_index("dp")
    c = me % 2
    x = (me // 2) % 2
    z = me // 4
    xp = me + 2 - 4 * x
    cp = me + 1 - 2 * c

    def rows(b):
        return pl.ds(pl.multiple_of(b * tb, tb), tb)

    def span(d):
        return pl.ds(pl.multiple_of(d * chunk, chunk), chunk)

    def block(zz, xx, cc):
        return zz * 4 + xx * 2 + cc

    def remote(src, dst, send, recv, **where):
        return pltpu.make_async_remote_copy(
            src_ref=src, dst_ref=dst, send_sem=send, recv_sem=recv,
            device_id=where, device_id_type=MESH,
        )

    barrier = pltpu.get_barrier_semaphore()
    for partner in (xp, cp):
        pl.semaphore_signal(barrier, inc=1, device_id={"expert": partner}, device_id_type=MESH)

    @pl.when(z > 0)
    def _():
        pl.semaphore_signal(barrier, inc=1, device_id={"expert": me - 4}, device_id_type=MESH)

    @pl.when(z < nz - 1)
    def _():
        pl.semaphore_signal(barrier, inc=1, device_id={"expert": me + 4}, device_id_type=MESH)

    for j in range(1, m):
        pl.semaphore_signal(barrier, inc=1, device_id={"dp": (dp + j) % m}, device_id_type=MESH)
    my_rows = pl.ds(pl.multiple_of(dp * dl, dl), dl)
    local = [
        pltpu.make_async_copy(src, dst, local_s.at[i])
        for i, (src, dst) in enumerate(
            (
                (tok, pay.at[rows(me), 0:d_all]),
                (og, pay.at[rows(me), d_all : 2 * d_all]),
                (gw.at[0], gu.at[my_rows, 0:hid]),
                (uw.at[0], gu.at[my_rows, hid:]),
                (dw.at[0], dn.at[:, my_rows]),
            )
        )
    ]
    for copy in local:
        copy.start()
    ids = ids_t[...].T
    rw = rw_t[...].T
    lane = lax.broadcasted_iota(jnp.int32, (tb, LANES), 1)
    lane_mod = jnp.where(lane < HALF, lane, lane - HALF)
    dense = jnp.zeros((tb, LANES), F32)
    for k in range(top):
        dense = dense + jnp.where(ids[:, k : k + 1] == lane_mod, rw[:, k : k + 1], 0.0)
    hi = dense.astype(BF16).astype(F32)
    pay[rows(me), 2 * d_all :] = jnp.where(lane < HALF, hi, dense - hi).astype(BF16)

    lines = jnp.minimum(z, 1) + jnp.minimum(nz - 1 - z, 1)
    pl.semaphore_wait(barrier, 1 + m + lines)

    def weight_copies(peer, owner, which=(0, 1, 2)):
        own = pl.ds(pl.multiple_of(owner * dl, dl), dl)
        ends = (
            (gw.at[0], gu.at[own, 0:hid]),
            (uw.at[0], gu.at[own, hid:]),
            (dw.at[0], dn.at[:, own]),
        )
        return [
            remote(*ends[i], wsend_s.at[peer, i], wrecv_s.at[owner, i], dp=peer) for i in which
        ]

    half = tb // 2

    def gather_copy(b, h, sem, to):
        at = pl.ds(pl.multiple_of(b * tb + h * half, half), half)
        return remote(pay.at[at], pay.at[at], sem, brecv_s.at[b, h], expert=to)

    def up(zz, h):
        return gather_copy(block(zz, x, c), h, usend_s.at[zz, h], me + 4)

    def down(zz, h):
        return gather_copy(block(zz, x, c), h, dsend_s.at[zz, h], me - 4)

    def across(zz, h):
        return gather_copy(block(zz, x, c), h, xsend_s.at[zz, h], xp)

    def core(zz, xx, h):
        return gather_copy(block(zz, xx, c), h, csend_s.at[zz * 2 + xx, h], cp)

    def arrived(b, h):
        gather_copy(b, h, xsend_s.at[0, 0], xp).wait_recv()

    for copy in local[:2]:
        copy.wait()
    for h in range(2):

        @pl.when(z < nz - 1)
        def _():
            up(z, h).start()

        @pl.when(z > 0)
        def _():
            down(z, h).start()

        across(z, h).start()
        core(z, x, h).start()
    for j in range(1, m):
        for copy in weight_copies((dp + j) % m, dp, (0, 1)):
            copy.start()

    def partner_half(zz, h):
        arrived(block(zz, 1 - x, c), h)
        core(zz, 1 - x, h).start()

    def partner_blocks(s):
        for h in range(2):

            @pl.when(s == 0)
            def _():
                partner_half(z, h)

            @pl.when((s > 0) & (z - s >= 0))
            def _():
                partner_half(z - s, h)

            @pl.when((s > 0) & (z + s < nz))
            def _():
                partner_half(z + s, h)

    def gather_step(s, carry):
        for h in range(2):

            @pl.when(z - s >= 0)
            def _():
                arrived(block(z - s, x, c), h)

                @pl.when(z < nz - 1)
                def _():
                    up(z - s, h).start()

                across(z - s, h).start()
                core(z - s, x, h).start()

            @pl.when(z + s < nz)
            def _():
                arrived(block(z + s, x, c), h)

                @pl.when(z > 0)
                def _():
                    down(z + s, h).start()

                across(z + s, h).start()
                core(z + s, x, h).start()

        partner_blocks(s - 1)
        return carry

    lax.fori_loop(1, nz - 1, gather_step, 0)
    for j in range(1, m):
        weight_copies((dp + j) % m, dp, (2,))[0].start()
    gather_step(nz - 1, 0)

    below, above = z, nz - 1 - z
    upward = jnp.minimum(jnp.maximum(above - below, 0), 1)
    excess = jnp.maximum(above - below, below - above)
    paired = jnp.minimum(above, below)

    def order(p):
        inner = jnp.minimum(jnp.maximum(p - excess + 1, 0), 1)
        q = jnp.maximum(p - excess, 0)
        near = z + (paired - q // 2) * (1 - 2 * (q % 2)) * (2 * upward - 1)
        far = upward * (nz - 1 - p) + (1 - upward) * p
        return inner * near + (1 - inner) * far

    wide = lax.broadcasted_iota(jnp.int32, (chunk, LANES), 1)
    mine_hi = wide == me
    mine_lo = wide == me + HALF

    def chunk_weight(r):
        weights = pay[span(r), 2 * d_all :].astype(F32)
        return jnp.sum(jnp.where(mine_hi | mine_lo, weights, 0.0), 1, keepdims=True)

    def act_step(p, carry):
        r = order(nz - 1 - p)
        for h in range(2):
            arrived(block(r, 0, 1 - c), h)
            arrived(block(r, 1, 1 - c), h)
        act = jnp.dot(pay[span(r), 0:d_all], gu[...], preferred_element_type=F32)
        gate_act, up_act = act[:, 0:hid], act[:, hid:]
        sig = jax.nn.sigmoid(gate_act)
        silu = gate_act * sig
        hidden = silu * up_act
        hh[span(r), :] = hidden.astype(BF16)
        scaled = (chunk_weight(r) * hidden).astype(BF16)
        hw[span(r), :] = scaled
        if split:
            hw_t[:, span(r)] = scaled.T
            x_t[:, span(r)] = pay[span(r), 0:d_all].T
        gb[span(r), 0:hid] = (up_act * sig * (1.0 + gate_act * (1.0 - sig))).astype(BF16)
        gb[span(r), hid:] = silu.astype(BF16)
        return carry

    for copy in local[2:]:
        copy.wait()
    for j in range(1, m):
        other = (dp + j) % m
        for copy in weight_copies(other, other, (0, 1)):
            copy.wait_recv()
    if split:

        def turn_step(i, carry):
            at = pl.ds(pl.multiple_of(i * 256, 256), 256)
            gu_t[:, at] = gu[at, :].T
            return carry

        lax.fori_loop(0, d_all // 256, turn_step, 0)
        dn_t[my_rows, :] = dn[:, my_rows].T
    lax.fori_loop(0, nz - 1, act_step, 0)
    partner_blocks(nz - 1)
    act_step(nz - 1, 0)

    def gather_sends(zz, carry):
        for h in range(2):

            @pl.when((z < nz - 1) & (zz <= z))
            def _():
                up(zz, h).wait_send()

            @pl.when((z > 0) & (zz >= z))
            def _():
                down(zz, h).wait_send()

            across(zz, h).wait_send()
            core(zz, 0, h).wait_send()
            core(zz, 1, h).wait_send()
        return carry

    def back_step(p, carry):
        r = order(p)
        grads = pay[span(r), d_all : 2 * d_all]
        if split:
            raw = jnp.dot(grads, dn_t[...], preferred_element_type=F32)
        else:
            raw = lax.dot_general(grads, dn[...], LAST, preferred_element_type=F32)
        back = chunk_weight(r) * raw
        route = jnp.sum(hh[span(r), :].astype(F32) * raw, 1, keepdims=True)
        route_hi = route.astype(BF16).astype(F32)
        yb[span(r), 2 * d_all :] = jnp.where(
            mine_hi, route_hi, jnp.where(mine_lo, route - route_hi, 0.0)
        ).astype(BF16)
        gb[span(r), 0:hid] = (back * gb[span(r), 0:hid].astype(F32)).astype(BF16)
        gb[span(r), hid:] = (back * gb[span(r), hid:].astype(F32)).astype(BF16)
        return carry

    piece = min(256, dl)
    pieces = dl // piece
    depth = min(total, 1024)

    def contract(left, right):
        def part(i):
            at = pl.ds(i * depth, depth) if isinstance(i, int) else pl.ds(pl.multiple_of(i * depth, depth), depth)
            return lax.dot_general(left(at), right(at), ROWS, preferred_element_type=F32)

        if total == depth:
            return part(0)
        return lax.fori_loop(1, total // depth, lambda i, acc: acc + part(i), part(0))

    def features(owner, i, shift):
        return pl.ds(pl.multiple_of(shift + owner * dl + i * piece, piece), piece)

    def gate_part(owner, i):
        if split:
            return jnp.dot(x_t[features(owner, i, 0), :], gb[...], preferred_element_type=F32)
        return contract(lambda at: pay[at, features(owner, i, 0)], lambda at: gb[at, :])

    def down_part(owner):
        mine = pl.ds(pl.multiple_of(d_all + owner * dl, dl), dl)
        if split:
            return jnp.dot(hw_t[...], pay[:, mine], preferred_element_type=F32)
        return contract(lambda at: hw[at, :], lambda at: pay[at, mine])

    def cut(i):
        return pl.ds(pl.multiple_of(i * piece, piece), piece)

    def gate_copy(peer, owner, i):
        return remote(
            gstage.at[peer, cut(i)], grecv.at[owner, cut(i)],
            gsend_s.at[peer, i], grecv_s.at[owner, i], dp=peer,
        )

    def down_copy(peer, owner):
        return remote(dstage.at[peer], drecv.at[owner], qsend_s.at[peer], qrecv_s.at[owner], dp=peer)

    def down_share(t, carry):
        peer = (dp + 1 + t) % m
        dstage[peer] = down_part(peer).astype(BF16)
        down_copy(peer, dp).start()
        return carry

    def gate_share(t, carry):
        peer = (dp + 1 + t // pieces) % m
        i = t % pieces
        gstage[peer, cut(i)] = gate_part(peer, i).astype(BF16)
        gate_copy(peer, dp, i).start()
        return carry

    def gate_own(i, carry):
        own = gate_part(dp, i)
        gg[0, cut(i), :] = own[:, 0:hid]
        ug[0, cut(i), :] = own[:, hid:]
        return carry

    def core_back(d, xx):
        return remote(
            yb.at[rows(block(d, xx, 1 - c))], crecv.at[d * 2 + xx],
            c2send_s.at[d * 2 + xx], c2recv_s.at[d * 2 + xx], expert=cp,
        )

    def across_back(d):
        return remote(yb.at[rows(block(d, 1 - x, c))], xrecv.at[d], x2send_s.at[d], x2recv_s.at[d], expert=xp)

    def half_rows(b, h):
        return pl.ds(pl.multiple_of(b * tb + h * half, half), half)

    def line_back(d, slot, h, to):
        return remote(
            yb.at[half_rows(block(d, x, c), h)], zrecv.at[slot, pl.ds(h * half, half)],
            z2send_s.at[d, h], z2recv_s.at[slot, h], expert=to,
        )

    def add(b, got):
        yb[rows(b), :] = (yb[rows(b), :].astype(F32) + got[...].astype(F32)).astype(BF16)

    def out_step(p, carry):
        d = order(p)
        yb[span(d), 0:d_all] = jnp.dot(hw[span(d), :], dn[...], preferred_element_type=F32).astype(BF16)
        if split:
            back = jnp.dot(gb[span(d), :], gu_t[...], preferred_element_type=F32)
        else:
            back = lax.dot_general(gb[span(d), :], gu[...], LAST, preferred_element_type=F32)
        yb[span(d), d_all : 2 * d_all] = back.astype(BF16)
        core_back(d, 0).start()
        core_back(d, 1).start()
        return carry

    def across_step(p, carry):
        d = order(p)
        core_back(d, 0).wait_recv()
        core_back(d, 1).wait_recv()
        add(block(d, 0, c), crecv.at[d * 2])
        add(block(d, 1, c), crecv.at[d * 2 + 1])
        across_back(d).start()
        return carry

    def take_line(d, slot, h):
        line_back(d, slot, h, xp).wait_recv()
        at = half_rows(block(d, x, c), h)
        got = zrecv[slot, pl.ds(h * half, half), :]
        yb[at, :] = (yb[at, :].astype(F32) + got.astype(F32)).astype(BF16)

    def line_step(p, carry):
        d = order(p)
        across_back(d).wait_recv()
        add(block(d, x, c), xrecv.at[d])
        for h in range(2):

            @pl.when(d < z)
            def _():
                @pl.when(z < nz - 1)
                def _():
                    take_line(d, d, h)

                line_back(d, d, h, me - 4).start()

            @pl.when(d > z)
            def _():
                @pl.when(z > 0)
                def _():
                    take_line(d, d, h)

                @pl.when(d > z + 1)
                def _():
                    line_back(d, d, h, me + 4).start()

                @pl.when(d == z + 1)
                def _():
                    line_back(d, nz, h, me + 4).start()

        return carry

    for j in range(1, m):
        other = (dp + j) % m
        weight_copies(other, other, (2,))[0].wait_recv()
        if split:
            theirs = pl.ds(pl.multiple_of(other * dl, dl), dl)
            dn_t[theirs, :] = dn[:, theirs].T

    if split:

        def more_step(p, carry):
            out_step(p, carry)
            return across_step(p, carry)

        back_step(0, 0)
        out_step(0, 0)
        lax.fori_loop(0, m - 1, down_share, 0)
        across_step(0, 0)
        back_step(1, 0)
        more_step(1, 0)
        lax.fori_loop(2, nz, back_step, 0)
        lax.fori_loop(0, (m - 1) * pieces, gate_share, 0)
        lax.fori_loop(2, nz, more_step, 0)
        line_step(0, 0)
        dg[0] = down_part(dp)
        line_step(1, 0)
        lax.fori_loop(0, pieces, gate_own, 0)
        lax.fori_loop(2, nz, line_step, 0)
    else:
        lax.fori_loop(0, m - 1, down_share, 0)
        lax.fori_loop(0, nz, gather_sends, 0)
        lax.fori_loop(0, nz, back_step, 0)
        lax.fori_loop(0, (m - 1) * pieces, gate_share, 0)
        dg[0] = down_part(dp)
        lax.fori_loop(0, pieces, gate_own, 0)
        lax.fori_loop(0, nz, out_step, 0)
        lax.fori_loop(0, nz, across_step, 0)
        lax.fori_loop(0, nz, line_step, 0)

    @pl.when(z < nz - 1)
    def _():
        take_line(z, z, 0)
        take_line(z, z, 1)

    @pl.when(z > 0)
    def _():
        take_line(z, nz, 0)
        take_line(z, nz, 1)

    lo_ref[...] = yb[rows(me), 0:d_all]
    tg_ref[...] = yb[rows(me), d_all : 2 * d_all]
    route = yb[rows(me), 2 * d_all :].astype(F32)
    slot = lax.broadcasted_iota(jnp.int32, (tb, top), 1)
    picked = jnp.zeros((tb, top), F32)
    for k in range(top):
        value = jnp.sum(jnp.where(ids[:, k : k + 1] == lane_mod, route, 0.0), 1, keepdims=True)
        picked = jnp.where(slot == k, value, picked)
    rg_ref[...] = picked.T

    def share_end(t, carry):
        peer = (dp + 1 + t // pieces) % m
        i = t % pieces
        gate_copy(peer, peer, i).wait()
        gg[0, cut(i), :] += grecv[peer, cut(i), 0:hid].astype(F32)
        ug[0, cut(i), :] += grecv[peer, cut(i), hid:].astype(F32)
        return carry

    def down_end(t, carry):
        peer = (dp + 1 + t) % m
        down_copy(peer, peer).wait()
        dg[0] += drecv[peer].astype(F32)
        return carry

    lax.fori_loop(0, m - 1, down_end, 0)
    lax.fori_loop(0, (m - 1) * pieces, share_end, 0)

    for j in range(1, m):
        for copy in weight_copies((dp + j) % m, dp):
            copy.wait_send()
    if split:
        lax.fori_loop(0, nz, gather_sends, 0)

    def sends_end(d, carry):
        core_back(d, 0).wait_send()
        core_back(d, 1).wait_send()
        across_back(d).wait_send()

        @pl.when(d != z)
        def _():
            line_back(d, d, 0, xp).wait_send()
            line_back(d, d, 1, xp).wait_send()

        return carry

    lax.fori_loop(0, nz, sends_end, 0)


def hand_over(count, *refs):
    ins, outs, held = refs[:count], refs[count : 2 * count], refs[2 * count : 3 * count]
    sems = refs[-1]
    loads = [pltpu.make_async_copy(ins[i], held[i], sems.at[0, i]) for i in range(count)]
    stores = [pltpu.make_async_copy(held[i], outs[i], sems.at[1, i]) for i in range(count)]
    for load in loads:
        load.start()
    for load, store in zip(loads, stores):
        load.wait()
        store.start()
    for store in stores:
        store.wait()


def shards(tokens, expert_ids, route_weight, out_grad, gate_weight, up_weight, down_weight):
    tb, d_all = tokens.shape
    dl, hid = gate_weight.shape[1:]
    n, m = lax.axis_size("expert"), lax.axis_size("dp")
    nz = n // 4
    total = n * tb
    width = 2 * d_all + LANES
    piece = min(256, dl)
    pieces = dl // piece
    dma = pltpu.SemaphoreType.DMA
    vmem = pl.BlockSpec(memory_space=pltpu.VMEM)
    anywhere = pl.BlockSpec(memory_space=pl.ANY)
    split = total * width * 2 <= 8 * 1024 * 1024
    results = (
        pl.pallas_call(
            functools.partial(kernel, n, m, split),
            out_shape=(
                jax.ShapeDtypeStruct((tb, d_all), BF16),
                jax.ShapeDtypeStruct((tb, d_all), BF16),
                jax.ShapeDtypeStruct(expert_ids.shape[::-1], F32),
                jax.ShapeDtypeStruct((1, dl, hid), F32),
                jax.ShapeDtypeStruct((1, dl, hid), F32),
                jax.ShapeDtypeStruct((1, hid, dl), F32),
            ),
            in_specs=[anywhere, vmem, vmem] + [anywhere] * 4,
            out_specs=tuple([vmem] * 6),
            scratch_shapes=[
                pltpu.VMEM((total, width), BF16),
                pltpu.VMEM((d_all, 2 * hid), BF16),
                pltpu.VMEM((hid, d_all), BF16),
                pltpu.VMEM((total, 2 * hid), BF16),
                pltpu.VMEM((total, hid), BF16),
                pltpu.VMEM((total, hid), BF16),
                pltpu.VMEM((2 * nz, tb, width), BF16),
                pltpu.VMEM((nz, tb, width), BF16),
                pltpu.VMEM((nz + 1, tb, width), BF16),
                pltpu.VMEM((m, dl, 2 * hid), BF16),
                pltpu.VMEM((m, dl, 2 * hid), BF16),
                pltpu.VMEM((m, hid, dl), BF16),
                pltpu.VMEM((m, hid, dl), BF16),
                dma((n, 2)), dma((nz, 2)), dma((nz, 2)), dma((nz, 2)), dma((2 * nz, 2)), dma((m, 3)), dma((m, 3)),
                dma((m, pieces)), dma((m, pieces)), dma((m,)), dma((m,)), dma((5,)),
                dma((2 * nz,)), dma((2 * nz,)), dma((nz,)), dma((nz,)), dma((nz, 2)), dma((nz + 1, 2)),
            ]
            + (
                [
                    pltpu.VMEM((total, width), BF16),
                    pltpu.VMEM((2 * hid, d_all), BF16),
                    pltpu.VMEM((d_all, hid), BF16),
                    pltpu.VMEM((d_all, total), BF16),
                    pltpu.VMEM((hid, total), BF16),
                ]
                if split
                else []
            ),
            compiler_params=pltpu.CompilerParams(
                collective_id=0, has_side_effects=True, vmem_limit_bytes=60 * 1024 * 1024
            ),
        )(tokens, expert_ids.T, route_weight.T, out_grad, gate_weight, up_weight, down_weight)
    )
    layer_out, token_grad, route_grad, *grads = pl.pallas_call(
        functools.partial(hand_over, len(results)),
        out_shape=tuple(jax.ShapeDtypeStruct(r.shape, r.dtype) for r in results),
        in_specs=[anywhere] * len(results),
        out_specs=tuple([anywhere] * len(results)),
        scratch_shapes=[pltpu.VMEM(r.shape, r.dtype) for r in results] + [dma((2, len(results)))],
        compiler_params=pltpu.CompilerParams(vmem_limit_bytes=60 * 1024 * 1024),
    )(*results)
    return (layer_out, token_grad, route_grad.T, *grads)


def solution(mesh):
    rows = P(("dp", "expert"), None)
    return jax.shard_map(
        shards,
        mesh=mesh,
        in_specs=(rows, rows, rows, rows, P("expert", "dp", None), P("expert", "dp", None), P("expert", None, "dp")),
        out_specs=(rows, rows, rows, P("expert", "dp", None), P("expert", "dp", None), P("expert", None, "dp")),
        check_vma=False,
    )
```
